128 devices in a mesh: member: 32 (over z_lo, y, x), space: 4 (over z_hi, core).
Axes of the slice: x: 4, y: 4, z: 4 (z_hi: 2, z_lo: 2; z = z_hi * 2 + z_lo), core: 2. Of those that a mesh axis runs over, the one named last changes fastest.
Arguments:
- prior_realizations: bfloat16 [64, 73, 49152], P('member', None, 'space'), may hold values from -6 to 6
- expand_projection_matrix: bfloat16 [2, 512, 73], replicated, may hold values from -0.75 to 0.75
- contract_projection_matrix: bfloat16 [2, 73, 512], replicated, may hold values from -0.25 to 0.25
- obs_site: int32 [128, 512], P(('member', 'space')), may hold values from 0 to 46719
- obs_count: int32 [128], P(('member', 'space')), may hold values from 128 to 512, as said below
- obs_value: float32 [128, 512], P(('member', 'space')), may hold values from -5 to 5
- obs_weight: float32 [128, 512], P(('member', 'space')), may hold values from 0.05 to 1
Outputs:
- increments: bfloat16 [64, 73, 49152], P('member', None, 'space')
The draws below stay inside these ranges and needn't reach their ends.
Inputs may be any that keep to these rules, and one draw needn't show every extreme that they name: `obs_count`: in every draw some tile has all 512 slots live.
All inputs are finite; a program needn't handle non-finite values.
Results may differ from the reference program's by a relative error of at most 0.0072.
Values may be sent and summed in bfloat16 or wider, within the bound.
A program may use at most 128 MiB of HBM per device.

```python
import math
import jax
import jax.numpy as jnp
from jax import lax

FIELD_VARIABLES = 73
HID = 512
LAYERS = 2
CT = 384
HALO = 128
OBS_CAP = 512
REALIZATION_NUM = 64
LATITUDE_POINTS = 12288
CELLS = 49152
EXT = 640
TILES = 128
N_MEMBER = 32
N_SPACE = 4


def draw_obs_count(key, part):
    key = jax.random.fold_in(key, 7)
    first_key, second_key = jax.random.split(key)
    base = jax.random.randint(first_key, (TILES,), OBS_CAP // 4, OBS_CAP + 1)
    fullest = jax.random.randint(second_key, (), 0, TILES)
    return jnp.where(jnp.arange(TILES) == fullest, OBS_CAP, base).astype(jnp.int32)


def touch_ends(drawn, rng, smallest, high):
    shape = drawn.shape
    index_at = [jax.random.randint(jax.random.fold_in(rng, axis), (), 0, shape[axis]) for axis in range(len(shape))]
    drawn = drawn.at[tuple(index_at)].set(smallest)
    longest = shape.index(max(shape))
    index_at[longest] = (index_at[longest] + 1) % shape[longest]
    return drawn.at[tuple(index_at)].set(high)


def level_of(stream_key, shape, cuts, least, largest):
    def one(dim, shards_of):
        heights = jax.random.uniform(jax.random.fold_in(jax.random.fold_in(stream_key, 6), dim), (shards_of,), jnp.float32, least / len(cuts), largest / len(cuts))
        return jnp.repeat(jnp.exp(heights), shape[dim] // shards_of).reshape((-1,) + (1,) * (len(shape) - dim - 1))

    level = one(*cuts[0])
    for cut in cuts[1:]:
        level = level * one(*cut)
    return level


def centred(key, extent, scale, reach, cuts=(), kind=jnp.bfloat16):
    result = scale * jax.random.normal(key, extent, jnp.float32)
    if cuts:
        result = result * level_of(key, extent, cuts, -0.22, 0.18)
    return jnp.clip(result, -reach, reach).astype(kind)


def setup_inputs(seed: int = 0) -> dict:
    keys = jax.random.split(jax.random.key(seed), 8)
    return {
        "prior_realizations": centred(keys[0], (REALIZATION_NUM, FIELD_VARIABLES, CELLS), 1.0, 6.0, ((0, 32), (2, 4))),
        "expand_projection_matrix": centred(keys[1], (LAYERS, HID, FIELD_VARIABLES), FIELD_VARIABLES ** -0.5, 0.75),
        "contract_projection_matrix": centred(keys[2], (LAYERS, FIELD_VARIABLES, HID), HID ** -0.5, 0.25),
        "obs_site": touch_ends(jax.random.randint(keys[3], (TILES, OBS_CAP), 0, FIELD_VARIABLES * EXT), jax.random.fold_in(keys[3], 1), 0, (FIELD_VARIABLES * EXT) - 1).astype(jnp.int32),
        "obs_count": draw_obs_count(jax.random.fold_in(keys[7], 71), 0),
        "obs_value": centred(keys[5], (TILES, OBS_CAP), 1.0, 5.0, ((0, 128),), jnp.float32),
        "obs_weight": jnp.clip(jnp.exp(math.log(1.0) - 2.9957323 * jax.random.uniform(keys[6], (TILES, OBS_CAP), jnp.float32) ** level_of(keys[6], (TILES, OBS_CAP), ((0, 128),), -0.2, 0.2)), 0.05, 1.0),
    }


def march_one_interval(fields, expand_projection_matrix, contract_projection_matrix):
    current = fields.astype(jnp.float32)
    for layer_idx in range(expand_projection_matrix.shape[0]):
        center = current - lax.optimization_barrier(jnp.mean(current, axis=1, keepdims=True))
        spread = lax.optimization_barrier(jnp.mean(center * center, axis=1, keepdims=True))
        normed = (center * lax.rsqrt(spread + 1e-06)).astype(jnp.bfloat16)
        lifted = jnp.einsum('hc,gcn->ghn', expand_projection_matrix[layer_idx].astype(jnp.float32), normed.astype(jnp.float32))
        hidden = jax.nn.gelu(lifted).astype(jnp.bfloat16)
        current = current + jnp.einsum('ch,ghn->gcn', contract_projection_matrix[layer_idx].astype(jnp.float32), hidden.astype(jnp.float32))
    return current.astype(jnp.bfloat16)

def live_mask(place_row, live_count, tile_pos, tile_total, tile_len, margin):
    strip_spot = place_row % (tile_len + 2 * margin)
    slot_live = jnp.arange(place_row.shape[0], dtype=jnp.int32) < live_count
    low_edge = (strip_spot < margin) & (tile_pos == 0)
    high_edge = (strip_spot >= margin + tile_len) & (tile_pos == tile_total - 1)
    return slot_live & jnp.logical_not(low_edge) & jnp.logical_not(high_edge)

def analyse(observed, own_cells, value_row, weight_row, live_slots):
    members = observed.shape[0]
    highest = lax.Precision.HIGHEST
    obs_mean = lax.optimization_barrier(jnp.mean(observed, axis=0))
    spread = observed - obs_mean
    departure = value_row - obs_mean
    rate = jnp.where(live_slots, weight_row, jnp.zeros_like(weight_row))
    scaled = spread * rate
    gram_matrix = jnp.dot(scaled, spread.T, precision=highest)
    drive = jnp.dot(scaled, departure, precision=highest)
    system = gram_matrix + (members - 1) * jnp.eye(members, dtype=jnp.float32)
    factor = jnp.linalg.cholesky(system)
    right_side = jnp.concatenate([drive[:, None], gram_matrix], axis=1)
    first_pass = lax.linalg.triangular_solve(factor, right_side, left_side=True, lower=True)
    solved = lax.linalg.triangular_solve(factor, first_pass, left_side=True, lower=True, transpose_a=True)
    mixing = solved[:, :1] - 0.5 * solved[:, 1:]
    field_f = own_cells.astype(jnp.float32)
    anomaly = field_f - lax.optimization_barrier(jnp.mean(field_f, axis=0, keepdims=True))
    return jnp.einsum('jk,jcn->kcn', mixing, anomaly, precision=highest).astype(jnp.bfloat16)

def reference(prior_realizations, expand_projection_matrix, contract_projection_matrix, obs_site, obs_count, obs_value, obs_weight):
    prediction_module = lax.map(lambda lone_realization: march_one_interval(lone_realization[None], expand_projection_matrix, contract_projection_matrix)[0], prior_realizations)
    latitude_partition = prediction_module.reshape(REALIZATION_NUM, FIELD_VARIABLES, N_SPACE, LATITUDE_POINTS)
    padded = jnp.pad(latitude_partition, ((0, 0), (0, 0), (0, 0), (HALO, HALO)))

    def one_tile(inputs):
        tile_id, place_row, live_count, value_row, weight_row = inputs
        tile_pos = (tile_id // N_SPACE).astype(jnp.int32)
        band_idx = (tile_id % N_SPACE).astype(jnp.int32)
        zero_idx = jnp.zeros((), jnp.int32)
        strip_full = lax.dynamic_slice(padded, (zero_idx, zero_idx, band_idx, (tile_pos * CT).astype(jnp.int32)), (REALIZATION_NUM, FIELD_VARIABLES, 1, EXT))[:, :, 0]
        own_cells = strip_full[:, :, HALO:HALO + CT]
        observed = jnp.take(strip_full.reshape(REALIZATION_NUM, FIELD_VARIABLES * EXT), place_row, axis=1).astype(jnp.float32)
        live_slots = live_mask(place_row, live_count, tile_pos, N_MEMBER, CT, HALO)
        return analyse(observed, own_cells, value_row, weight_row, live_slots)
    tile_ids = jnp.arange(TILES, dtype=jnp.int32)
    per_tile = lax.map(one_tile, (tile_ids, obs_site, obs_count, obs_value, obs_weight))
    per_tile = per_tile.reshape(N_MEMBER, N_SPACE, REALIZATION_NUM, FIELD_VARIABLES, CT)
    return jnp.transpose(per_tile, (2, 3, 1, 0, 4)).reshape(REALIZATION_NUM, FIELD_VARIABLES, CELLS)
```

```python
import functools
import math

import jax
import jax.numpy as jnp
from jax import lax
from jax.experimental import pallas as pl
from jax.experimental.pallas import tpu as pltpu
from jax.sharding import PartitionSpec as P

MESH = pl.DeviceIdType.MESH
F32 = jnp.float32
BF16 = jnp.bfloat16

CH = 73
TILE = 384
HALO = 128
STRIP = TILE + 2 * HALO
SLOTS = 512
MEMBERS = 64
PEERS = 32
PITCH = 80
LANES = 128
BLOCKS = TILE // LANES
ROWS = 448
GELU_A = math.sqrt(2.0 / math.pi)
GELU_B = GELU_A * 0.044715


def peer_of(me, step):
    off = lax.rem(step * ORDER, PEERS)
    x = lax.rem(lax.rem(me, 4) + lax.rem(off, 4), 4)
    y = lax.rem(lax.rem(me // 4, 4) + lax.rem(off // 4, 4), 4)
    z = lax.rem(me // 16 + off // 16, 2)
    return z * 16 + y * 4 + x


ORDER = 25


def layer(x, w_up, w_down):
    mean = jnp.sum(x, axis=0, keepdims=True) * (1.0 / CH)
    center = x - mean
    var = jnp.sum(center * center, axis=0, keepdims=True) * (1.0 / CH)
    normed = (center * lax.rsqrt(var + 1e-06)).astype(BF16)
    lifted = jnp.dot(w_up, normed, preferred_element_type=F32)
    bend = jnp.tanh(lifted * (GELU_A + GELU_B * (lifted * lifted)))
    half = 0.5 * lifted
    hidden = (half + half * bend).astype(BF16)
    return x + jnp.dot(w_down, hidden, preferred_element_type=F32)


def pack_message(blocks, msg, slot):
    for b, block in enumerate(blocks):
        msg[slot, b * 64 : b * 64 + 64, :] = block[:64].astype(BF16)
    for b in range(0, 2 * BLOCKS, 2):
        pair = jnp.concatenate([blocks[b][64:72], blocks[b + 1][64:72]], axis=0)
        msg[slot, 384 + 8 * b : 400 + 8 * b, :] = pair.astype(BF16)
    last = [block[72:73] for block in blocks]
    last.append(jnp.zeros((16 - 2 * BLOCKS, LANES), F32))
    msg[slot, 432:448, :] = jnp.concatenate(last, axis=0).astype(BF16)


def kernel(
    prior,
    w_up,
    w_down,
    site,
    count,
    value,
    weight,
    out,
    msg1,
    got1,
    msg2,
    got2,
    state,
    code_own,
    code_out,
    code_in,
    smem_own,
    smem_in,
    obs_own,
    obs_out,
    obs_in,
    send1,
    recv1,
    send2,
    recv2,
    near_send,
    near_recv,
    local_sem,
):
    me = lax.axis_index("member")
    left = lax.rem(me + PEERS - 1, PEERS)
    right = lax.rem(me + 1, PEERS)

    barrier = pltpu.get_barrier_semaphore()

    def greet(step, carry):
        pl.semaphore_signal(
            barrier, inc=1, device_id={"member": peer_of(me, step)}, device_id_type=MESH
        )
        return carry

    lax.fori_loop(1, PEERS, greet, 0)

    sites = site[...]
    channel = ((sites >> 7) * 6554) >> 15
    spot = sites - channel * STRIP
    slot_id = lax.broadcasted_iota(jnp.int32, (1, SLOTS), 1)

    def code(cell):
        row = (cell >> 7) * (MEMBERS * PITCH) + channel
        return row * LANES + ((slot_id - cell) & (LANES - 1))

    code_own[...] = code(jnp.clip(spot - HALO, 0, TILE - 1))
    code_out[0] = code(jnp.minimum(spot, HALO - 1) + (TILE - HALO))
    code_out[1] = code(jnp.maximum(spot - (HALO + TILE), 0))

    own_codes = pltpu.make_async_copy(code_own, smem_own, local_sem.at[0])
    own_codes.start()

    pl.semaphore_wait(barrier, PEERS - 1)

    def near_copy(src, dst, sem, target):
        return pltpu.make_async_remote_copy(
            src_ref=src,
            dst_ref=dst,
            send_sem=near_send.at[sem],
            recv_sem=near_recv.at[sem],
            device_id={"member": target},
            device_id_type=MESH,
        )

    code_left = near_copy(code_out.at[0], code_in.at[0], 0, left)
    code_right = near_copy(code_out.at[1], code_in.at[1], 1, right)
    code_left.start()
    code_right.start()

    def exchange(msg, got, send, recv, target, source):
        return pltpu.make_async_remote_copy(
            src_ref=msg.at[target],
            dst_ref=got.at[source],
            send_sem=send.at[target],
            recv_sem=recv.at[source],
            device_id={"member": target},
            device_id_type=MESH,
        )

    def forecast(target):
        start = pl.multiple_of(target * TILE, TILE)
        x = jnp.concatenate(
            [prior[m, :, pl.ds(start, TILE)].astype(F32) for m in range(2)], axis=1
        )
        for l in range(2):
            x = layer(x, w_up[l], w_down[l])
        pack_message(
            [x[:, b * LANES : (b + 1) * LANES] for b in range(2 * BLOCKS)], msg1, target
        )

    def forecast_step(i, carry):
        target = peer_of(me, i)
        forecast(target)
        exchange(msg1, got1, send1, recv1, target, me).start()
        return carry

    lax.fori_loop(1, PEERS, forecast_step, 0)
    forecast(me)
    own_tile = pltpu.make_async_copy(msg1.at[me], got1.at[me], local_sem.at[1])
    own_tile.start()

    code_left.wait()
    code_right.wait()
    in_codes = pltpu.make_async_copy(code_in, smem_in, local_sem.at[2])
    in_codes.start()

    def unpack(source):
        tail = got1[source, 384:448, :].astype(F32)
        for m in range(2):
            for j in range(BLOCKS):
                b = m * BLOCKS + j
                base = pl.multiple_of(j * (MEMBERS * PITCH) + (2 * source + m) * PITCH, 8)
                state[pl.ds(base, 64), :] = got1[source, b * 64 : b * 64 + 64, :].astype(F32)
                state[pl.ds(base + 64, 8), :] = tail[8 * b : 8 * b + 8]
                state[pl.ds(base + 72, 1), :] = tail[48 + b : 49 + b]

    own_tile.wait()
    unpack(me)

    def receive_step(i, carry):
        source = source_of(me, i)
        exchange(msg1, got1, send1, recv1, source, source).wait_recv()
        unpack(source)
        return carry

    lax.fori_loop(1, PEERS, receive_step, 0)

    own_codes.wait()
    in_codes.wait()

    lane = lax.broadcasted_iota(jnp.int32, (MEMBERS, LANES), 1)

    def gather(read_code, group):
        def one(p, acc):
            word = read_code(group * LANES + p)
            slab = state[pl.ds(word >> 7, MEMBERS, stride=PITCH), :]
            moved = pltpu.roll(slab, word & (LANES - 1), 1)
            return jnp.where(lane == p, moved, acc)

        return lax.fori_loop(
            0, LANES, one, jnp.zeros((MEMBERS, LANES), F32), unroll=8
        )

    for g in range(SLOTS // LANES):
        span = slice(g * LANES, (g + 1) * LANES)
        obs_out[0, :, span] = gather(lambda p: smem_in[1, 0, p], g).astype(BF16)
        obs_out[1, :, span] = gather(lambda p: smem_in[0, 0, p], g).astype(BF16)
    obs_left = near_copy(obs_out.at[0], obs_in.at[0], 2, left)
    obs_right = near_copy(obs_out.at[1], obs_in.at[1], 3, right)
    obs_left.start()
    obs_right.start()
    for g in range(SLOTS // LANES):
        span = slice(g * LANES, (g + 1) * LANES)
        obs_own[:, span] = gather(lambda p: smem_own[0, p], g)
    obs_left.wait()
    obs_right.wait()

    below = spot < HALO
    above = spot >= HALO + TILE
    observed = jnp.where(
        below,
        obs_in[1].astype(F32),
        jnp.where(above, obs_in[0].astype(F32), obs_own[...]),
    )
    live = slot_id < count[0]
    live = live & jnp.logical_not(below & (me == 0))
    live = live & jnp.logical_not(above & (me == PEERS - 1))
    rate = jnp.where(live, weight[...], 0.0)
    obs_mean = jnp.sum(observed, axis=0, keepdims=True) * (1.0 / MEMBERS)
    spread = observed - obs_mean
    departure = value[...] - obs_mean
    scaled = spread * rate
    right_side = jnp.concatenate(
        [spread, jnp.broadcast_to(departure, (MEMBERS, SLOTS))], axis=0
    )
    gram_drive = lax.dot_general(
        scaled,
        right_side,
        (((1,), (1,)), ((), ())),
        precision=lax.Precision.HIGHEST,
        preferred_element_type=F32,
    )
    row_id = lax.broadcasted_iota(jnp.int32, (MEMBERS, 2 * MEMBERS), 0)
    col_id = lax.broadcasted_iota(jnp.int32, (MEMBERS, 2 * MEMBERS), 1)
    swapped = pltpu.roll(gram_drive, MEMBERS, 1)
    system = jnp.where(
        col_id < MEMBERS,
        jnp.where(row_id == col_id, gram_drive + (MEMBERS - 1.0), gram_drive),
        gram_drive - 0.5 * swapped,
    )
    for j in range(MEMBERS):
        pivot_row = system[j : j + 1, :]
        pivot_row = pivot_row / system[j : j + 1, j : j + 1]
        column = system[:, j : j + 1]
        system = jnp.where(row_id == j, pivot_row, system - column * pivot_row)
    mixing = system[:, MEMBERS:]
    mixing = mixing - jnp.sum(mixing, axis=0, keepdims=True) * (1.0 / MEMBERS)
    mixing_t = mixing.T
    coarse = mixing_t.astype(BF16)
    fine = (mixing_t - coarse.astype(F32)).astype(BF16)
    mixer = jnp.concatenate([coarse, fine], axis=1)

    def mix(c, carry):
        rows = [pl.ds(j * (MEMBERS * PITCH) + c, MEMBERS, stride=PITCH) for j in range(BLOCKS)]
        slab = jnp.concatenate([state[r, :] for r in rows], axis=1).astype(BF16)
        mixed = jnp.dot(
            mixer, jnp.concatenate([slab, slab], axis=0), preferred_element_type=F32
        )
        for j, r in enumerate(rows):
            state[r, :] = mixed[:, j * LANES : (j + 1) * LANES]
        return carry

    lax.fori_loop(0, CH, mix, 0)

    def pack_for(target):
        blocks = []
        for m in range(2):
            for j in range(BLOCKS):
                base = pl.multiple_of(j * (MEMBERS * PITCH) + (2 * target + m) * PITCH, 8)
                blocks.append(state[pl.ds(base, CH), :])
        pack_message(blocks, msg2, target)

    def send_step(i, carry):
        target = peer_of(me, i)
        pack_for(target)
        exchange(msg2, got2, send2, recv2, target, me).start()
        return carry

    lax.fori_loop(1, PEERS, send_step, 0)
    pack_for(me)

    def place(got, source):
        start = pl.multiple_of(source * TILE, TILE)
        tail = got[source, 384:448, :].astype(F32)
        for m in range(2):
            for j in range(BLOCKS):
                b = m * BLOCKS + j
                span = pl.ds(pl.multiple_of(start + j * LANES, LANES), LANES)
                out[m, 0:64, span] = got[source, b * 64 : b * 64 + 64, :]
                rest = jnp.concatenate([tail[8 * b : 8 * b + 8], tail[48 + b : 49 + b]], axis=0)
                out[m, 64:CH, span] = rest.astype(BF16)

    place(msg2, me)

    def place_step(i, carry):
        source = source_of(me, i)
        exchange(msg2, got2, send2, recv2, source, source).wait_recv()
        place(got2, source)
        return carry

    lax.fori_loop(1, PEERS, place_step, 0)

    def sent_step(i, carry):
        target = peer_of(me, i)
        exchange(msg1, got1, send1, recv1, target, me).wait_send()
        exchange(msg2, got2, send2, recv2, target, me).wait_send()
        return carry

    lax.fori_loop(1, PEERS, sent_step, 0)


def source_of(me, step):
    off = lax.rem(step * ORDER, PEERS)
    x = lax.rem(lax.rem(me, 4) + 4 - lax.rem(off, 4), 4)
    y = lax.rem(lax.rem(me // 4, 4) + 4 - lax.rem(off // 4, 4), 4)
    z = lax.rem(me // 16 + off // 16, 2)
    return z * 16 + y * 4 + x


def local(prior, w_up, w_down, site, count, value, weight):
    vmem = pl.BlockSpec(memory_space=pltpu.VMEM)
    smem = pl.BlockSpec(memory_space=pltpu.SMEM)
    return pl.pallas_call(
        kernel,
        out_shape=jax.ShapeDtypeStruct(prior.shape, BF16),
        in_specs=[vmem, vmem, vmem, vmem, smem, vmem, vmem],
        out_specs=vmem,
        scratch_shapes=[
            pltpu.VMEM((PEERS, ROWS, LANES), BF16),
            pltpu.VMEM((PEERS, ROWS, LANES), BF16),
            pltpu.VMEM((PEERS, ROWS, LANES), BF16),
            pltpu.VMEM((PEERS, ROWS, LANES), BF16),
            pltpu.VMEM((BLOCKS * MEMBERS * PITCH, LANES), F32),
            pltpu.VMEM((1, SLOTS), jnp.int32),
            pltpu.VMEM((2, 1, SLOTS), jnp.int32),
            pltpu.VMEM((2, 1, SLOTS), jnp.int32),
            pltpu.SMEM((1, SLOTS), jnp.int32),
            pltpu.SMEM((2, 1, SLOTS), jnp.int32),
            pltpu.VMEM((MEMBERS, SLOTS), F32),
            pltpu.VMEM((2, MEMBERS, SLOTS), BF16),
            pltpu.VMEM((2, MEMBERS, SLOTS), BF16),
            pltpu.SemaphoreType.DMA((PEERS,)),
            pltpu.SemaphoreType.DMA((PEERS,)),
            pltpu.SemaphoreType.DMA((PEERS,)),
            pltpu.SemaphoreType.DMA((PEERS,)),
            pltpu.SemaphoreType.DMA((4,)),
            pltpu.SemaphoreType.DMA((4,)),
            pltpu.SemaphoreType.DMA((3,)),
        ],
        compiler_params=pltpu.CompilerParams(
            collective_id=0, has_side_effects=True, vmem_limit_bytes=56 << 20
        ),
    )(prior, w_up, w_down, site, count, value, weight)


def solution(mesh):
    in_specs = (
        P("member", None, "space"),
        P(),
        P(),
        P(("member", "space"), None),
        P(("member", "space")),
        P(("member", "space"), None),
        P(("member", "space"), None),
    )
    return jax.shard_map(
        local,
        mesh=mesh,
        in_specs=in_specs,
        out_specs=P("member", None, "space"),
        check_vma=False,
    )
```

```python
import functools
import math

import jax
import jax.numpy as jnp
from jax import lax
from jax.experimental import pallas as pl
from jax.experimental.pallas import tpu as pltpu
from jax.sharding import PartitionSpec as P

MESH = pl.DeviceIdType.MESH
F32 = jnp.float32
BF16 = jnp.bfloat16

CH = 73
TILE = 384
HALO = 128
STRIP = TILE + 2 * HALO
SLOTS = 512
MEMBERS = 64
PEERS = 32
FILL = 80
PAIR = 152
HID = 512
LANES = 128
BLOCKS = TILE // LANES
ORDER = 25
GROUP = 4
HALVES = 38
GELU_A = math.sqrt(2.0 / math.pi)
GELU_B = GELU_A * 0.044715


def peer_of(me, step):
    off = lax.rem(step * ORDER, PEERS)
    x = lax.rem(lax.rem(me, 4) + lax.rem(off, 4), 4)
    y = lax.rem(lax.rem(me // 4, 4) + lax.rem(off // 4, 4), 4)
    z = lax.rem(me // 16 + off // 16, 2)
    return z * 16 + y * 4 + x


def normalise(x):
    groups = x.reshape(PAIR // 8, 8, x.shape[1])

    def over_channels(group):
        group = group + pltpu.roll(group, 4, 0)
        return (group + pltpu.roll(group, 2, 0)) * (1.0 / CH)

    center = groups - over_channels(jnp.sum(groups, axis=0))[None]
    row = lax.broadcasted_iota(jnp.int32, center.shape[1:], 0)
    last = jnp.where(row < 2, center[PAIR // 8 - 1], 0.0)
    center = jnp.concatenate([center[: PAIR // 8 - 1], last[None]], axis=0)
    var = over_channels(jnp.sum(center * center, axis=0))
    return (center * lax.rsqrt(var + 1e-06)[None]).reshape(x.shape).astype(BF16)


def layer(x, w_up, w_down):
    lifted = jnp.dot(w_up, normalise(x), preferred_element_type=F32)
    bend = jnp.tanh(lifted * (GELU_A + GELU_B * (lifted * lifted)))
    twice_hidden = (lifted + lifted * bend).astype(BF16)
    return x + 0.5 * jnp.dot(w_down, twice_hidden, preferred_element_type=F32)


def kernel(
    prior,
    w_up,
    w_down,
    site,
    count,
    value,
    weight,
    out,
    fields,
    msg,
    state,
    mixed,
    flipped,
    rows_own,
    spread_w,
    up,
    down,
    code_own,
    code_out,
    code_in,
    smem_own,
    smem_in,
    obs_out,
    obs_in,
    load_sem,
    exchange_sem,
    near_send,
    near_recv,
    local_sem,
):
    me = lax.axis_index("member")
    left = lax.rem(me + PEERS - 1, PEERS)
    right = lax.rem(me + 1, PEERS)

    def tile_span(tile, j):
        return pl.ds(pl.multiple_of(tile * TILE + j * LANES, LANES), LANES)

    def load_pair(i, sem):
        for t in range(2):
            for j in range(BLOCKS):
                pltpu.make_async_copy(
                    prior.at[:, :, tile_span(peer_of(me, 2 * i + 1 + t), j)],
                    fields.at[i, t * BLOCKS + j, 0:CH],
                    load_sem.at[sem],
                ).start()

    def loaded(span, sem):
        block = fields.at[span, :, 0:CH]
        return pltpu.make_async_copy(block, block, load_sem.at[sem])

    load_pair(0, 0)

    def load_step(i, carry):
        load_pair(i, 1)
        return carry

    lax.fori_loop(1, PEERS // 2, load_step, 0)

    barrier = pltpu.get_barrier_semaphore()

    def greet(step, carry):
        pl.semaphore_signal(
            barrier, inc=1, device_id={"member": peer_of(me, step)}, device_id_type=MESH
        )
        return carry

    lax.fori_loop(1, PEERS, greet, 0)

    sites = site[...]
    channel = ((sites >> 7) * 6554) >> 15
    spot = sites - channel * STRIP

    def code(cell):
        row = ((cell >> 7) * HALVES + (channel >> 1)) * LANES + (cell & (LANES - 1))
        return 2 * row + (channel & 1)

    code_own[...] = code(jnp.clip(spot - HALO, 0, TILE - 1))
    code_out[0] = code(jnp.minimum(spot, HALO - 1) + (TILE - HALO))
    code_out[1] = code(jnp.maximum(spot - (HALO + TILE), 0))

    own_codes = pltpu.make_async_copy(code_own, smem_own, local_sem.at[0])
    own_codes.start()

    state[:, CH:FILL] = jnp.zeros((BLOCKS, FILL - CH, PEERS, 2, LANES), BF16)

    spread_w[...] = jnp.zeros_like(spread_w)
    for source, l in ((w_up, 0), (w_up, 1), (w_down, 0), (w_down, 1)):
        plain = source[:, l, :].astype(F32)
        for m in range(2):
            for b in range(HID // LANES):
                spread_w[m * 4 + b, pl.ds(m, CH, stride=2), :] = plain[:, b * LANES : (b + 1) * LANES]
        for b in range(2 * HID // LANES):
            span = slice(b * LANES, (b + 1) * LANES)
            if source is w_up:
                up[l, span, :] = spread_w[b].T.astype(BF16)
            else:
                down[l, :, span] = spread_w[b, 0:160].astype(BF16)

    def near_copy(src, dst, sem, target):
        return pltpu.make_async_remote_copy(
            src_ref=src,
            dst_ref=dst,
            send_sem=near_send.at[sem],
            recv_sem=near_recv.at[sem],
            device_id={"member": target},
            device_id_type=MESH,
        )

    code_left = near_copy(code_out.at[0], code_in.at[0], 0, left)
    code_right = near_copy(code_out.at[1], code_in.at[1], 1, right)
    def gather_copy(target, source):
        return pltpu.make_async_remote_copy(
            src_ref=msg.at[target, :, 0:CH],
            dst_ref=state.at[:, 0:CH, source],
            send_sem=exchange_sem.at[0],
            recv_sem=exchange_sem.at[1],
            device_id={"member": target},
            device_id_type=MESH,
        )

    def forecast(i, tiles):
        row = lax.broadcasted_iota(jnp.int32, (PAIR, LANES), 0)
        blocks = []
        for b in range(2 * BLOCKS):
            block = fields.at[i, b].reshape(2 * FILL, LANES)[0:PAIR, :].astype(F32)
            blocks.append(jnp.where(row < 2 * CH, block, 0.0))
        x = jnp.concatenate(blocks, axis=1)
        for l in range(2):
            x = layer(x, up[l, :, 0:PAIR], down[l, 0:PAIR])
        fill = jnp.zeros((2 * FILL - PAIR, LANES), F32)
        for t, tile in enumerate(tiles):
            for j in range(BLOCKS):
                b = t * BLOCKS + j
                block = jnp.concatenate([x[:, b * LANES : (b + 1) * LANES], fill], axis=0)
                msg.at[tile, j].reshape(2 * FILL, LANES)[...] = block.astype(BF16)

    def forecast_step(i, carry):
        tiles = (peer_of(me, 2 * i + 1), peer_of(me, 2 * i + 2))

        @pl.when(i == 0)
        def _():
            loaded(pl.ds(0, 1), 0).wait()

        @pl.when(i == 1)
        def _():
            loaded(pl.ds(1, PEERS // 2 - 1), 1).wait()

        forecast(i, tiles)

        @pl.when(i == 0)
        def _():
            pl.semaphore_wait(barrier, PEERS - 1)
            code_left.start()
            code_right.start()

        gather_copy(tiles[0], me).start()

        @pl.when(i < PEERS // 2 - 1)
        def _():
            gather_copy(tiles[1], me).start()

        return carry

    lax.fori_loop(0, PEERS // 2, forecast_step, 0)
    own_tile = pltpu.make_async_copy(msg.at[me, :, 0:CH], state.at[:, 0:CH, me], local_sem.at[1])
    own_tile.start()

    code_left.wait()
    code_right.wait()
    in_codes = pltpu.make_async_copy(code_in, smem_in, local_sem.at[2])
    in_codes.start()
    own_codes.wait()
    in_codes.wait()
    own_tile.wait()

    others = msg.at[0 : PEERS - 1, :, 0:CH]
    all_members = pltpu.make_async_remote_copy(
        src_ref=others,
        dst_ref=others,
        send_sem=exchange_sem.at[0],
        recv_sem=exchange_sem.at[1],
        device_id={"member": left},
        device_id_type=MESH,
    )
    all_members.wait_recv()

    row_id = lax.broadcasted_iota(jnp.int32, (LANES, LANES), 0)
    col_id = lax.broadcasted_iota(jnp.int32, (LANES, LANES), 1)
    unit = jnp.where(row_id == col_id, 1.0, 0.0).astype(BF16)

    def flip(rows):
        return lax.dot_general(
            unit, rows, (((1,), (1,)), ((), ())), preferred_element_type=F32
        )

    def flip_step(g, carry):
        for j in range(BLOCKS):
            slabs = state.at[j, pl.ds(g * GROUP, GROUP)].reshape(GROUP * MEMBERS, LANES)[...]
            turned = flip(slabs)
            for h in range(GROUP // 2):
                base = pl.multiple_of((j * HALVES + g * (GROUP // 2) + h) * LANES, LANES)
                flipped[pl.ds(base, LANES), :] = turned[:, h * LANES : (h + 1) * LANES]
        return carry

    lax.fori_loop(0, HALVES * 2 // GROUP, flip_step, 0)

    UNROLL = 16

    def gather(read_code, codes):
        def one(i, carry):
            for u in range(UNROLL):
                p = i * UNROLL + u
                rows_own[pl.ds(p, 1), :] = flipped[pl.ds(read_code(p) >> 1, 1), :]
            return carry

        lax.fori_loop(0, SLOTS // UNROLL, one, 0)
        both = flip(rows_own[...].astype(BF16))
        return jnp.where((codes & 1) == 0, both[:MEMBERS], both[MEMBERS:])

    obs_left = near_copy(obs_out.at[0], obs_in.at[0], 2, left)
    obs_right = near_copy(obs_out.at[1], obs_in.at[1], 3, right)
    obs_out[0] = gather(lambda p: smem_in[1, 0, p], code_in[1]).astype(BF16)
    obs_left.start()
    obs_out[1] = gather(lambda p: smem_in[0, 0, p], code_in[0]).astype(BF16)
    obs_right.start()
    obs_own = gather(lambda p: smem_own[0, p], code_own[...])
    obs_left.wait()
    obs_right.wait()

    below = spot < HALO
    above = spot >= HALO + TILE
    observed = jnp.where(
        below,
        obs_in[1].astype(F32),
        jnp.where(above, obs_in[0].astype(F32), obs_own),
    )
    slot_id = lax.broadcasted_iota(jnp.int32, (1, SLOTS), 1)
    live = slot_id < count[0]
    live = live & jnp.logical_not(below & (me == 0))
    live = live & jnp.logical_not(above & (me == PEERS - 1))
    rate = jnp.where(live, weight[...], 0.0)
    obs_mean = jnp.sum(observed, axis=0, keepdims=True) * (1.0 / MEMBERS)
    spread = observed - obs_mean
    departure = value[...] - obs_mean
    scaled = spread * rate
    right_side = jnp.concatenate(
        [spread, jnp.broadcast_to(departure, (MEMBERS, SLOTS))], axis=0
    )
    gram_drive = lax.dot_general(
        scaled,
        right_side,
        (((1,), (1,)), ((), ())),
        precision=lax.Precision.HIGHEST,
        preferred_element_type=F32,
    )
    row_id = lax.broadcasted_iota(jnp.int32, (MEMBERS, 2 * MEMBERS), 0)
    col_id = lax.broadcasted_iota(jnp.int32, (MEMBERS, 2 * MEMBERS), 1)
    swapped = pltpu.roll(gram_drive, MEMBERS, 1)
    system = jnp.where(
        col_id < MEMBERS,
        jnp.where(row_id == col_id, gram_drive + (MEMBERS - 1.0), gram_drive),
        gram_drive - 0.5 * swapped,
    )

    def eliminate(i, system):
        for j in range(0, 8, 2):
            row0, row1 = system[j : j + 1, :], system[j + 1 : j + 2, :]
            a, b = row0[:, j : j + 1], row0[:, j + 1 : j + 2]
            c, d = row1[:, j : j + 1], row1[:, j + 1 : j + 2]
            scale = 1.0 / (a * d - b * c)
            new0 = (row0 * d - row1 * b) * scale
            new1 = (row1 * a - row0 * c) * scale
            rest = system - system[:, j : j + 1] * new0 - system[:, j + 1 : j + 2] * new1
            system = jnp.where(row_id == j, new0, jnp.where(row_id == j + 1, new1, rest))
        system = jnp.concatenate([system[8:], system[:8]], axis=0)
        return pltpu.roll(system, LANES - 8, 1)

    system = lax.fori_loop(0, MEMBERS // 8, eliminate, system)
    mixing = system[:, :MEMBERS]
    mixing = mixing - jnp.sum(mixing, axis=0, keepdims=True) * (1.0 / MEMBERS)
    mixing_t = mixing.T
    coarse = mixing_t.astype(BF16)
    fine = (mixing_t - coarse.astype(F32)).astype(BF16)
    mixer = jnp.concatenate([coarse, fine], axis=1)

    def mix(j, channels):
        slabs = [state.at[j, c].reshape(MEMBERS, LANES)[...] for c in channels]
        slab = jnp.concatenate(slabs, axis=1)
        result = jnp.dot(
            mixer, jnp.concatenate([slab, slab], axis=0), preferred_element_type=F32
        ).astype(BF16)
        for k, c in enumerate(channels):
            mixed.at[j, c].reshape(MEMBERS, LANES)[...] = result[:, k * LANES : (k + 1) * LANES]

    def scatter_copy(j, target, tile):
        return pltpu.make_async_remote_copy(
            src_ref=mixed.at[j, 0:CH, target],
            dst_ref=out.at[:, :, tile_span(tile, j)],
            send_sem=exchange_sem.at[2],
            recv_sem=exchange_sem.at[3],
            device_id={"member": target},
            device_id_type=MESH,
        )

    def own_block(j):
        return pltpu.make_async_copy(
            mixed.at[j, 0:CH, me], out.at[:, :, tile_span(me, j)], local_sem.at[3 + j]
        )

    WIDE = 8
    for j in range(BLOCKS):

        def mix_step(i, carry):
            mix(j, [i * WIDE + k for k in range(WIDE)])
            return carry

        lax.fori_loop(0, FILL // WIDE, mix_step, 0)

        def send_step(i, carry):
            scatter_copy(j, peer_of(me, i), me).start()
            return carry

        lax.fori_loop(1, PEERS, send_step, 0)
        own_block(j).start()

    all_members.wait_send()
    for j in range(BLOCKS):
        own_block(j).wait()
    others = out.at[:, :, 0 : (PEERS - 1) * TILE]
    pltpu.make_async_remote_copy(
        src_ref=others,
        dst_ref=others,
        send_sem=exchange_sem.at[2],
        recv_sem=exchange_sem.at[3],
        device_id={"member": left},
        device_id_type=MESH,
    ).wait()


def copy_kernel(source, target, sem):
    copy = pltpu.make_async_copy(source, target, sem)
    copy.start()
    copy.wait()


def local(prior, w_up, w_down, site, count, value, weight):
    vmem = pl.BlockSpec(memory_space=pltpu.VMEM)
    smem = pl.BlockSpec(memory_space=pltpu.SMEM)
    anywhere = pl.BlockSpec(memory_space=pl.ANY)
    members, channels, cells = prior.shape
    result = pl.pallas_call(
        kernel,
        out_shape=jax.ShapeDtypeStruct((channels, members, cells), BF16),
        in_specs=[anywhere, vmem, vmem, vmem, smem, vmem, vmem],
        out_specs=anywhere,
        scratch_shapes=[
            pltpu.VMEM((PEERS // 2, 2 * BLOCKS, FILL, 2, LANES), BF16),
            pltpu.VMEM((PEERS, BLOCKS, FILL, 2, LANES), BF16),
            pltpu.VMEM((BLOCKS, FILL, PEERS, 2, LANES), BF16),
            pltpu.VMEM((BLOCKS, FILL, PEERS, 2, LANES), BF16),
            pltpu.VMEM((BLOCKS * HALVES * LANES, LANES), F32),
            pltpu.VMEM((SLOTS, LANES), F32),
            pltpu.VMEM((2 * HID // LANES, 2 * LANES, LANES), F32),
            pltpu.VMEM((2, 2 * HID, 2 * LANES), BF16),
            pltpu.VMEM((2, 160, 2 * HID), BF16),
            pltpu.VMEM((1, SLOTS), jnp.int32),
            pltpu.VMEM((2, 1, SLOTS), jnp.int32),
            pltpu.VMEM((2, 1, SLOTS), jnp.int32),
            pltpu.SMEM((1, SLOTS), jnp.int32),
            pltpu.SMEM((2, 1, SLOTS), jnp.int32),
            pltpu.VMEM((2, MEMBERS, SLOTS), BF16),
            pltpu.VMEM((2, MEMBERS, SLOTS), BF16),
            pltpu.SemaphoreType.DMA((2,)),
            pltpu.SemaphoreType.DMA((4,)),
            pltpu.SemaphoreType.DMA((4,)),
            pltpu.SemaphoreType.DMA((4,)),
            pltpu.SemaphoreType.DMA((3 + BLOCKS,)),
        ],
        compiler_params=pltpu.CompilerParams(
            collective_id=0, has_side_effects=True, vmem_limit_bytes=56 << 20
        ),
    )(
        prior.transpose(1, 0, 2),
        w_up.transpose(2, 0, 1),
        w_down.transpose(1, 0, 2),
        site,
        count,
        value,
        weight,
    )
    result = pl.pallas_call(
        copy_kernel,
        out_shape=jax.ShapeDtypeStruct(result.shape, BF16),
        in_specs=[vmem],
        out_specs=anywhere,
        scratch_shapes=[pltpu.SemaphoreType.DMA],
        compiler_params=pltpu.CompilerParams(vmem_limit_bytes=16 << 20),
    )(result)
    return result.transpose(1, 0, 2)


def solution(mesh):
    in_specs = (
        P("member", None, "space"),
        P(),
        P(),
        P(("member", "space"), None),
        P(("member", "space")),
        P(("member", "space"), None),
        P(("member", "space"), None),
    )
    return jax.shard_map(
        local,
        mesh=mesh,
        in_specs=in_specs,
        out_specs=P("member", None, "space"),
        check_vma=False,
    )
```

```python
import functools
import math

import jax
import jax.numpy as jnp
from jax import lax
from jax.experimental import pallas as pl
from jax.experimental.pallas import tpu as pltpu
from jax.sharding import PartitionSpec as P

MESH = pl.DeviceIdType.MESH
F32 = jnp.float32
BF16 = jnp.bfloat16

CH = 73
TILE = 384
HALO = 128
STRIP = TILE + 2 * HALO
SLOTS = 512
MEMBERS = 64
PEERS = 32
FILL = 80
PAIR = 152
HID = 512
LANES = 128
BLOCKS = TILE // LANES
ORDER = 25
COPY_ROWS = 8
GROUP = 4
HALVES = 40
GELU_A = math.sqrt(2.0 / math.pi)
GELU_B = GELU_A * 0.044715


def peer_of(me, step):
    off = lax.rem(step * ORDER, PEERS)
    x = lax.rem(lax.rem(me, 4) + lax.rem(off, 4), 4)
    y = lax.rem(lax.rem(me // 4, 4) + lax.rem(off // 4, 4), 4)
    z = lax.rem(me // 16 + off // 16, 2)
    return z * 16 + y * 4 + x


def normalise(x):
    groups = x.reshape(PAIR // 8, 8, x.shape[1])

    def over_channels(group):
        group = group + pltpu.roll(group, 4, 0)
        return (group + pltpu.roll(group, 2, 0)) * (1.0 / CH)

    center = groups - over_channels(jnp.sum(groups, axis=0))[None]
    row = lax.broadcasted_iota(jnp.int32, center.shape[1:], 0)
    last = jnp.where(row < 2, center[PAIR // 8 - 1], 0.0)
    center = jnp.concatenate([center[: PAIR // 8 - 1], last[None]], axis=0)
    var = over_channels(jnp.sum(center * center, axis=0))
    return (center * lax.rsqrt(var + 1e-06)[None]).reshape(x.shape).astype(BF16)


def layer(x, w_up, w_down):
    lifted = jnp.dot(w_up, normalise(x), preferred_element_type=F32)
    bend = jnp.tanh(lifted * (GELU_A + GELU_B * (lifted * lifted)))
    twice_hidden = (lifted + lifted * bend).astype(BF16)
    return x + 0.5 * jnp.dot(w_down, twice_hidden, preferred_element_type=F32)


def kernel(
    prior,
    w_up,
    w_down,
    site,
    count,
    value,
    weight,
    out,
    fields,
    msg,
    state,
    mixed,
    flipped,
    rows_own,
    spread_w,
    up,
    down,
    code_own,
    code_out,
    code_in,
    smem_own,
    smem_in,
    obs_out,
    obs_in,
    load_sem,
    exchange_sem,
    near_send,
    near_recv,
    local_sem,
):
    me = lax.axis_index("member")
    left = lax.rem(me + PEERS - 1, PEERS)
    right = lax.rem(me + 1, PEERS)

    def tile_span(tile, j):
        return pl.ds(pl.multiple_of(tile * TILE + j * LANES, LANES), LANES)

    def load_pair(i, sem):
        for t in range(2):
            for j in range(BLOCKS):
                pltpu.make_async_copy(
                    prior.at[:, :, tile_span(peer_of(me, 2 * i + 1 + t), j)],
                    fields.at[i, t * BLOCKS + j, 0:CH],
                    load_sem.at[sem],
                ).start()

    def loaded(i):
        block = fields.at[i, :, 0:CH]
        return pltpu.make_async_copy(block, block, load_sem.at[lax.rem(i, 2)])

    load_pair(0, 0)

    barrier = pltpu.get_barrier_semaphore()

    def greet(step, carry):
        pl.semaphore_signal(
            barrier, inc=1, device_id={"member": peer_of(me, step)}, device_id_type=MESH
        )
        return carry

    lax.fori_loop(1, PEERS, greet, 0)

    sites = site[...]
    channel = ((sites >> 7) * 6554) >> 15
    spot = sites - channel * STRIP

    def code(cell):
        row = ((cell >> 7) * HALVES + (channel >> 1)) * LANES + (cell & (LANES - 1))
        return 2 * row + (channel & 1)

    code_own[...] = code(jnp.clip(spot - HALO, 0, TILE - 1))
    code_out[0] = code(jnp.minimum(spot, HALO - 1) + (TILE - HALO))
    code_out[1] = code(jnp.maximum(spot - (HALO + TILE), 0))

    own_codes = pltpu.make_async_copy(code_own, smem_own, local_sem.at[0])
    own_codes.start()

    state[:, CH:FILL] = jnp.zeros((BLOCKS, FILL - CH, PEERS, 2, LANES), BF16)

    spread_w[...] = jnp.zeros_like(spread_w)
    for source, l in ((w_up, 0), (w_up, 1), (w_down, 0), (w_down, 1)):
        plain = source[:, l, :].astype(F32)
        for m in range(2):
            for b in range(HID // LANES):
                spread_w[m * 4 + b, pl.ds(m, CH, stride=2), :] = plain[:, b * LANES : (b + 1) * LANES]
        for b in range(2 * HID // LANES):
            span = slice(b * LANES, (b + 1) * LANES)
            if source is w_up:
                up[l, span, :] = spread_w[b].T.astype(BF16)
            else:
                down[l, :, span] = spread_w[b, 0:160].astype(BF16)

    def near_copy(src, dst, sem, target):
        return pltpu.make_async_remote_copy(
            src_ref=src,
            dst_ref=dst,
            send_sem=near_send.at[sem],
            recv_sem=near_recv.at[sem],
            device_id={"member": target},
            device_id_type=MESH,
        )

    code_left = near_copy(code_out.at[0], code_in.at[0], 0, left)
    code_right = near_copy(code_out.at[1], code_in.at[1], 1, right)
    def gather_copy(target, source):
        return pltpu.make_async_remote_copy(
            src_ref=msg.at[target, :, 0:CH],
            dst_ref=state.at[:, 0:CH, source],
            send_sem=exchange_sem.at[0],
            recv_sem=exchange_sem.at[1],
            device_id={"member": target},
            device_id_type=MESH,
        )

    def forecast(i, tiles):
        row = lax.broadcasted_iota(jnp.int32, (PAIR, LANES), 0)
        blocks = []
        for b in range(2 * BLOCKS):
            block = fields.at[i, b].reshape(2 * FILL, LANES)[0:PAIR, :].astype(F32)
            blocks.append(jnp.where(row < 2 * CH, block, 0.0))
        x = jnp.concatenate(blocks, axis=1)
        for l in range(2):
            x = layer(x, up[l, :, 0:PAIR], down[l, 0:PAIR])
        fill = jnp.zeros((2 * FILL - PAIR, LANES), F32)
        for t, tile in enumerate(tiles):
            for j in range(BLOCKS):
                b = t * BLOCKS + j
                block = jnp.concatenate([x[:, b * LANES : (b + 1) * LANES], fill], axis=0)
                msg.at[tile, j].reshape(2 * FILL, LANES)[...] = block.astype(BF16)

    def forecast_step(i, carry):
        tiles = (peer_of(me, 2 * i + 1), peer_of(me, 2 * i + 2))

        @pl.when(i < PEERS // 2 - 1)
        def _():
            load_pair(i + 1, lax.rem(i + 1, 2))

        loaded(i).wait()
        forecast(i, tiles)

        @pl.when(i == 0)
        def _():
            pl.semaphore_wait(barrier, PEERS - 1)
            code_left.start()
            code_right.start()

        gather_copy(tiles[0], me).start()

        @pl.when(i < PEERS // 2 - 1)
        def _():
            gather_copy(tiles[1], me).start()

        return carry

    lax.fori_loop(0, PEERS // 2, forecast_step, 0)
    own_tile = pltpu.make_async_copy(msg.at[me, :, 0:CH], state.at[:, 0:CH, me], local_sem.at[1])
    own_tile.start()

    code_left.wait()
    code_right.wait()
    in_codes = pltpu.make_async_copy(code_in, smem_in, local_sem.at[2])
    in_codes.start()
    own_codes.wait()
    in_codes.wait()
    own_tile.wait()

    others = msg.at[0 : PEERS - 1, :, 0:CH]
    all_members = pltpu.make_async_remote_copy(
        src_ref=others,
        dst_ref=others,
        send_sem=exchange_sem.at[0],
        recv_sem=exchange_sem.at[1],
        device_id={"member": left},
        device_id_type=MESH,
    )
    all_members.wait_recv()

    row_id = lax.broadcasted_iota(jnp.int32, (LANES, LANES), 0)
    col_id = lax.broadcasted_iota(jnp.int32, (LANES, LANES), 1)
    unit = jnp.where(row_id == col_id, 1.0, 0.0).astype(BF16)

    def flip(rows):
        return lax.dot_general(
            unit, rows, (((1,), (1,)), ((), ())), preferred_element_type=F32
        )

    def flip_block(j):
        def flip_step(g, carry):
            slabs = state.at[j, pl.ds(g * GROUP, GROUP)].reshape(GROUP * MEMBERS, LANES)[...]
            turned = flip(slabs)
            for h in range(GROUP // 2):
                base = pl.multiple_of((j * HALVES + g * (GROUP // 2) + h) * LANES, LANES)
                flipped[pl.ds(base, LANES), :] = turned[:, h * LANES : (h + 1) * LANES]
            return carry

        lax.fori_loop(0, HALVES * 2 // GROUP, flip_step, 0, unroll=4)

    UNROLL = 16

    def gather(read_code, codes):
        def one(i, carry):
            for u in range(UNROLL):
                p = i * UNROLL + u
                rows_own[pl.ds(p, 1), :] = flipped[pl.ds(read_code(p) >> 1, 1), :]
            return carry

        lax.fori_loop(0, SLOTS // UNROLL, one, 0)
        both = flip(rows_own[...].astype(BF16))
        return jnp.where((codes & 1) == 0, both[:MEMBERS], both[MEMBERS:])

    obs_left = near_copy(obs_out.at[0], obs_in.at[0], 2, left)
    obs_right = near_copy(obs_out.at[1], obs_in.at[1], 3, right)
    flip_block(0)
    obs_out[0] = gather(lambda p: smem_in[1, 0, p], code_in[1]).astype(BF16)
    obs_left.start()
    flip_block(BLOCKS - 1)
    obs_out[1] = gather(lambda p: smem_in[0, 0, p], code_in[0]).astype(BF16)
    obs_right.start()
    for j in range(1, BLOCKS - 1):
        flip_block(j)
    obs_own = gather(lambda p: smem_own[0, p], code_own[...])
    obs_left.wait()
    obs_right.wait()

    below = spot < HALO
    above = spot >= HALO + TILE
    observed = jnp.where(
        below,
        obs_in[1].astype(F32),
        jnp.where(above, obs_in[0].astype(F32), obs_own),
    )
    slot_id = lax.broadcasted_iota(jnp.int32, (1, SLOTS), 1)
    live = slot_id < count[0]
    live = live & jnp.logical_not(below & (me == 0))
    live = live & jnp.logical_not(above & (me == PEERS - 1))
    rate = jnp.where(live, weight[...], 0.0)
    obs_mean = jnp.sum(observed, axis=0, keepdims=True) * (1.0 / MEMBERS)
    spread = observed - obs_mean
    departure = value[...] - obs_mean
    scaled = spread * rate
    right_side = jnp.concatenate(
        [spread, jnp.broadcast_to(departure, (MEMBERS, SLOTS))], axis=0
    )
    gram_drive = lax.dot_general(
        scaled,
        right_side,
        (((1,), (1,)), ((), ())),
        precision=lax.Precision.HIGHEST,
        preferred_element_type=F32,
    )
    row_id = lax.broadcasted_iota(jnp.int32, (MEMBERS, 2 * MEMBERS), 0)
    col_id = lax.broadcasted_iota(jnp.int32, (MEMBERS, 2 * MEMBERS), 1)
    swapped = pltpu.roll(gram_drive, MEMBERS, 1)
    system = jnp.where(
        col_id < MEMBERS,
        jnp.where(row_id == col_id, gram_drive + (MEMBERS - 1.0), gram_drive),
        gram_drive - 0.5 * swapped,
    )

    def eliminate(i, system):
        sub = lax.broadcasted_iota(jnp.int32, (8, LANES), 0)
        for j in range(0, 8, 2):
            row0 = jnp.broadcast_to(system[0, j : j + 1, :], (8, LANES))
            row1 = jnp.broadcast_to(system[0, j + 1 : j + 2, :], (8, LANES))
            a = jnp.broadcast_to(row0[:, j : j + 1], (8, LANES))
            b = jnp.broadcast_to(row0[:, j + 1 : j + 2], (8, LANES))
            c = jnp.broadcast_to(row1[:, j : j + 1], (8, LANES))
            d = jnp.broadcast_to(row1[:, j + 1 : j + 2], (8, LANES))
            scale = 1.0 / (a * d - b * c)
            new0 = (row0 * d - row1 * b) * scale
            new1 = (row1 * a - row0 * c) * scale
            rest = system - system[:, :, j : j + 1] * new0 - system[:, :, j + 1 : j + 2] * new1
            first = jnp.where(sub == j, new0, jnp.where(sub == j + 1, new1, rest[0]))
            system = jnp.concatenate([first[None], rest[1:]], axis=0)
        system = jnp.concatenate([system[1:], system[:1]], axis=0)
        return pltpu.roll(system, LANES - 8, 2)

    system = lax.fori_loop(
        0, MEMBERS // 8, eliminate, system.reshape(MEMBERS // 8, 8, LANES)
    )
    mixing = system.reshape(MEMBERS, LANES)[:, :MEMBERS]
    mixing = mixing - jnp.sum(mixing, axis=0, keepdims=True) * (1.0 / MEMBERS)
    mixing_t = mixing.T
    coarse = mixing_t.astype(BF16)
    fine = (mixing_t - coarse.astype(F32)).astype(BF16)
    mixer = jnp.concatenate([coarse, fine], axis=1)

    def mix(j, channels):
        slabs = [state.at[j, c].reshape(MEMBERS, LANES)[...] for c in channels]
        slab = jnp.concatenate(slabs, axis=1)
        result = jnp.dot(
            mixer, jnp.concatenate([slab, slab], axis=0), preferred_element_type=F32
        ).astype(BF16)
        for k, c in enumerate(channels):
            mixed.at[j, c].reshape(MEMBERS, LANES)[...] = result[:, k * LANES : (k + 1) * LANES]

    def scatter_copy(j, target, tile):
        return pltpu.make_async_remote_copy(
            src_ref=mixed.at[j, 0:CH, target],
            dst_ref=out.at[:, :, tile_span(tile, j)],
            send_sem=exchange_sem.at[2],
            recv_sem=exchange_sem.at[3],
            device_id={"member": target},
            device_id_type=MESH,
        )

    def own_block(j):
        return pltpu.make_async_copy(
            mixed.at[j, 0:CH, me], out.at[:, :, tile_span(me, j)], local_sem.at[3 + j]
        )

    WIDE = 8
    for j in range(BLOCKS):

        def mix_step(i, carry):
            mix(j, [i * WIDE + k for k in range(WIDE)])
            return carry

        lax.fori_loop(0, FILL // WIDE, mix_step, 0)

        def send_step(i, carry):
            scatter_copy(j, peer_of(me, i), me).start()
            return carry

        lax.fori_loop(1, PEERS, send_step, 0)
        own_block(j).start()

    all_members.wait_send()
    for j in range(BLOCKS):
        own_block(j).wait()
    others = out.at[:, :, 0 : (PEERS - 1) * TILE]
    pltpu.make_async_remote_copy(
        src_ref=others,
        dst_ref=others,
        send_sem=exchange_sem.at[2],
        recv_sem=exchange_sem.at[3],
        device_id={"member": left},
        device_id_type=MESH,
    ).wait()


def copy_kernel(source, target, held, sem):
    spans = [pl.ds(c, min(COPY_ROWS, CH - c)) for c in range(0, CH, COPY_ROWS)]
    arrive = [
        pltpu.make_async_copy(source.at[span], held.at[span], sem.at[0, k])
        for k, span in enumerate(spans)
    ]
    leave = [
        pltpu.make_async_copy(held.at[span], target.at[span], sem.at[1, k])
        for k, span in enumerate(spans)
    ]
    for copy in arrive:
        copy.start()
    for k, copy in enumerate(leave):
        arrive[k].wait()
        copy.start()
    for copy in leave:
        copy.wait()


def local(prior, w_up, w_down, site, count, value, weight):
    vmem = pl.BlockSpec(memory_space=pltpu.VMEM)
    smem = pl.BlockSpec(memory_space=pltpu.SMEM)
    anywhere = pl.BlockSpec(memory_space=pl.ANY)
    members, channels, cells = prior.shape
    result = pl.pallas_call(
        kernel,
        out_shape=jax.ShapeDtypeStruct((channels, members, cells), BF16),
        in_specs=[anywhere, vmem, vmem, vmem, smem, vmem, vmem],
        out_specs=anywhere,
        scratch_shapes=[
            pltpu.VMEM((PEERS // 2, 2 * BLOCKS, FILL, 2, LANES), BF16),
            pltpu.VMEM((PEERS, BLOCKS, FILL, 2, LANES), BF16),
            pltpu.VMEM((BLOCKS, FILL, PEERS, 2, LANES), BF16),
            pltpu.VMEM((BLOCKS, FILL, PEERS, 2, LANES), BF16),
            pltpu.VMEM((BLOCKS * HALVES * LANES, LANES), F32),
            pltpu.VMEM((SLOTS, LANES), F32),
            pltpu.VMEM((2 * HID // LANES, 2 * LANES, LANES), F32),
            pltpu.VMEM((2, 2 * HID, 2 * LANES), BF16),
            pltpu.VMEM((2, 160, 2 * HID), BF16),
            pltpu.VMEM((1, SLOTS), jnp.int32),
            pltpu.VMEM((2, 1, SLOTS), jnp.int32),
            pltpu.VMEM((2, 1, SLOTS), jnp.int32),
            pltpu.SMEM((1, SLOTS), jnp.int32),
            pltpu.SMEM((2, 1, SLOTS), jnp.int32),
            pltpu.VMEM((2, MEMBERS, SLOTS), BF16),
            pltpu.VMEM((2, MEMBERS, SLOTS), BF16),
            pltpu.SemaphoreType.DMA((2,)),
            pltpu.SemaphoreType.DMA((4,)),
            pltpu.SemaphoreType.DMA((4,)),
            pltpu.SemaphoreType.DMA((4,)),
            pltpu.SemaphoreType.DMA((3 + BLOCKS,)),
        ],
        compiler_params=pltpu.CompilerParams(
            collective_id=0, has_side_effects=True, vmem_limit_bytes=56 << 20
        ),
    )(
        prior.transpose(1, 0, 2),
        w_up.transpose(2, 0, 1),
        w_down.transpose(1, 0, 2),
        site,
        count,
        value,
        weight,
    )
    result = pl.pallas_call(
        copy_kernel,
        out_shape=jax.ShapeDtypeStruct(result.shape, BF16),
        in_specs=[anywhere],
        out_specs=anywhere,
        scratch_shapes=[pltpu.VMEM(result.shape, BF16), pltpu.SemaphoreType.DMA((2, 10))],
        compiler_params=pltpu.CompilerParams(vmem_limit_bytes=56 << 20),
    )(result)
    return result.transpose(1, 0, 2)


def solution(mesh):
    in_specs = (
        P("member", None, "space"),
        P(),
        P(),
        P(("member", "space"), None),
        P(("member", "space")),
        P(("member", "space"), None),
        P(("member", "space"), None),
    )
    return jax.shard_map(
        local,
        mesh=mesh,
        in_specs=in_specs,
        out_specs=P("member", None, "space"),
        check_vma=False,
    )
```

```python
import functools
import math

import jax
import jax.numpy as jnp
from jax import lax
from jax.experimental import pallas as pl
from jax.experimental.pallas import tpu as pltpu
from jax.sharding import PartitionSpec as P

MESH = pl.DeviceIdType.MESH
F32 = jnp.float32
BF16 = jnp.bfloat16

CH = 73
TILE = 384
HALO = 128
STRIP = TILE + 2 * HALO
SLOTS = 512
MEMBERS = 64
PEERS = 32
FILL = 80
PAIR = 152
HID = 512
LANES = 128
BLOCKS = TILE // LANES
ORDER = 25
COPY_ROWS = 15
GROUP = 4
HALVES = 40
GELU_A = math.sqrt(2.0 / math.pi)
GELU_B = GELU_A * 0.044715


def peer_of(me, step):
    off = lax.rem(step * ORDER, PEERS)
    x = lax.rem(lax.rem(me, 4) + lax.rem(off, 4), 4)
    y = lax.rem(lax.rem(me // 4, 4) + lax.rem(off // 4, 4), 4)
    z = lax.rem(me // 16 + off // 16, 2)
    return z * 16 + y * 4 + x


def normalise(x):
    groups = x.reshape(PAIR // 8, 8, x.shape[1])

    def over_channels(group):
        group = group + pltpu.roll(group, 4, 0)
        return (group + pltpu.roll(group, 2, 0)) * (1.0 / CH)

    center = groups - over_channels(jnp.sum(groups, axis=0))[None]
    row = lax.broadcasted_iota(jnp.int32, center.shape[1:], 0)
    last = jnp.where(row < 2, center[PAIR // 8 - 1], 0.0)
    center = jnp.concatenate([center[: PAIR // 8 - 1], last[None]], axis=0)
    var = over_channels(jnp.sum(center * center, axis=0))
    return (center * lax.rsqrt(var + 1e-06)[None]).reshape(x.shape).astype(BF16)


def layer(x, w_up, w_down):
    lifted = jnp.dot(w_up, normalise(x), preferred_element_type=F32)
    bend = jnp.tanh(lifted * (GELU_A + GELU_B * (lifted * lifted)))
    twice_hidden = (lifted + lifted * bend).astype(BF16)
    return x + 0.5 * jnp.dot(w_down, twice_hidden, preferred_element_type=F32)


def kernel(
    prior,
    w_up_far,
    w_down_far,
    site_far,
    count,
    value_far,
    weight_far,
    out,
    w_up,
    w_down,
    site,
    value,
    weight,
    fields,
    msg,
    state,
    mixed,
    flipped,
    rows_own,
    spread_w,
    up,
    down,
    code_own,
    code_out,
    code_in,
    smem_own,
    smem_in,
    obs_out,
    obs_in,
    fetch_sem,
    load_sem,
    exchange_sem,
    near_send,
    near_recv,
    local_sem,
):
    fetches = [
        pltpu.make_async_copy(far, near, fetch_sem.at[k])
        for k, (far, near) in enumerate(
            (
                (site_far, site),
                (w_up_far, w_up),
                (w_down_far, w_down),
                (value_far, value),
                (weight_far, weight),
            )
        )
    ]
    for fetch in fetches:
        fetch.start()
    me = lax.axis_index("member")
    left = lax.rem(me + PEERS - 1, PEERS)
    right = lax.rem(me + 1, PEERS)

    def tile_span(tile, j):
        return pl.ds(pl.multiple_of(tile * TILE + j * LANES, LANES), LANES)

    def load_pair(i, sem):
        for t in range(2):
            for j in range(BLOCKS):
                pltpu.make_async_copy(
                    prior.at[:, :, tile_span(peer_of(me, 2 * i + 1 + t), j)],
                    fields.at[i, t * BLOCKS + j, 0:CH],
                    load_sem.at[sem],
                ).start()

    def loaded(i):
        block = fields.at[i, :, 0:CH]
        return pltpu.make_async_copy(block, block, load_sem.at[lax.rem(i, 2)])

    load_pair(0, 0)

    barrier = pltpu.get_barrier_semaphore()

    def greet(step, carry):
        pl.semaphore_signal(
            barrier, inc=1, device_id={"member": peer_of(me, step)}, device_id_type=MESH
        )
        return carry

    lax.fori_loop(1, PEERS, greet, 0)

    fetches[0].wait()
    sites = site[...]
    channel = ((sites >> 7) * 6554) >> 15
    spot = sites - channel * STRIP

    def code(cell):
        row = ((cell >> 7) * HALVES + (channel >> 1)) * LANES + (cell & (LANES - 1))
        return 2 * row + (channel & 1)

    code_own[...] = code(jnp.clip(spot - HALO, 0, TILE - 1))
    code_out[0] = code(jnp.minimum(spot, HALO - 1) + (TILE - HALO))
    code_out[1] = code(jnp.maximum(spot - (HALO + TILE), 0))

    own_codes = pltpu.make_async_copy(code_own, smem_own, local_sem.at[0])
    own_codes.start()

    state[:, CH:FILL] = jnp.zeros((BLOCKS, FILL - CH, PEERS, 2, LANES), BF16)

    spread_w[...] = jnp.zeros_like(spread_w)
    for fetch in fetches[1:]:
        fetch.wait()
    for source, l in ((w_up, 0), (w_down, 0), (w_up, 1), (w_down, 1)):
        plain = source[:, l, :].astype(F32)
        for m in range(2):
            for b in range(HID // LANES):
                spread_w[m * 4 + b, pl.ds(m, CH, stride=2), :] = plain[:, b * LANES : (b + 1) * LANES]
        for b in range(2 * HID // LANES):
            span = slice(b * LANES, (b + 1) * LANES)
            if source is w_up:
                up[l, span, :] = spread_w[b].T.astype(BF16)
            else:
                down[l, :, span] = spread_w[b, 0:160].astype(BF16)

    def near_copy(src, dst, sem, target):
        return pltpu.make_async_remote_copy(
            src_ref=src,
            dst_ref=dst,
            send_sem=near_send.at[sem],
            recv_sem=near_recv.at[sem],
            device_id={"member": target},
            device_id_type=MESH,
        )

    code_left = near_copy(code_out.at[0], code_in.at[0], 0, left)
    code_right = near_copy(code_out.at[1], code_in.at[1], 1, right)
    def gather_copy(target, source):
        return pltpu.make_async_remote_copy(
            src_ref=msg.at[target, :, 0:CH],
            dst_ref=state.at[:, 0:CH, source],
            send_sem=exchange_sem.at[0],
            recv_sem=exchange_sem.at[1],
            device_id={"member": target},
            device_id_type=MESH,
        )

    def forecast(i, tiles):
        row = lax.broadcasted_iota(jnp.int32, (PAIR, LANES), 0)
        blocks = []
        for b in range(2 * BLOCKS):
            block = fields.at[i, b].reshape(2 * FILL, LANES)[0:PAIR, :].astype(F32)
            blocks.append(jnp.where(row < 2 * CH, block, 0.0))
        x = jnp.concatenate(blocks, axis=1)
        for l in range(2):
            x = layer(x, up[l, :, 0:PAIR], down[l, 0:PAIR])
        fill = jnp.zeros((2 * FILL - PAIR, LANES), F32)
        for t, tile in enumerate(tiles):
            for j in range(BLOCKS):
                b = t * BLOCKS + j
                block = jnp.concatenate([x[:, b * LANES : (b + 1) * LANES], fill], axis=0)
                msg.at[tile, j].reshape(2 * FILL, LANES)[...] = block.astype(BF16)

    def forecast_step(i, carry):
        tiles = (peer_of(me, 2 * i + 1), peer_of(me, 2 * i + 2))

        @pl.when(i < PEERS // 2 - 1)
        def _():
            load_pair(i + 1, lax.rem(i + 1, 2))

        loaded(i).wait()
        forecast(i, tiles)

        @pl.when(i == 0)
        def _():
            pl.semaphore_wait(barrier, PEERS - 1)
            code_left.start()
            code_right.start()

        gather_copy(tiles[0], me).start()

        @pl.when(i < PEERS // 2 - 1)
        def _():
            gather_copy(tiles[1], me).start()

        return carry

    lax.fori_loop(0, PEERS // 2, forecast_step, 0)
    own_tile = pltpu.make_async_copy(msg.at[me, :, 0:CH], state.at[:, 0:CH, me], local_sem.at[1])
    own_tile.start()

    code_left.wait()
    code_right.wait()
    in_codes = pltpu.make_async_copy(code_in, smem_in, local_sem.at[2])
    in_codes.start()
    own_codes.wait()
    in_codes.wait()
    own_tile.wait()

    others = msg.at[0 : PEERS - 1, :, 0:CH]
    all_members = pltpu.make_async_remote_copy(
        src_ref=others,
        dst_ref=others,
        send_sem=exchange_sem.at[0],
        recv_sem=exchange_sem.at[1],
        device_id={"member": left},
        device_id_type=MESH,
    )
    all_members.wait_recv()

    row_id = lax.broadcasted_iota(jnp.int32, (LANES, LANES), 0)
    col_id = lax.broadcasted_iota(jnp.int32, (LANES, LANES), 1)
    unit = jnp.where(row_id == col_id, 1.0, 0.0).astype(BF16)

    def flip(rows):
        return lax.dot_general(
            unit, rows, (((1,), (1,)), ((), ())), preferred_element_type=F32
        )

    def flip_block(j):
        def flip_step(g, carry):
            slabs = state.at[j, pl.ds(g * GROUP, GROUP)].reshape(GROUP * MEMBERS, LANES)[...]
            for h in range(GROUP // 2):
                base = pl.multiple_of((j * HALVES + g * (GROUP // 2) + h) * LANES, LANES)
                pair = slabs[h * LANES : (h + 1) * LANES]
                flipped[pl.ds(base, LANES), :] = pair.T.astype(F32)
            return carry

        lax.fori_loop(0, HALVES * 2 // GROUP, flip_step, 0, unroll=5)

    UNROLL = 16

    def gather(read_code, codes):
        def one(i, carry):
            for u in range(UNROLL):
                p = i * UNROLL + u
                rows_own[pl.ds(p, 1), :] = flipped[pl.ds(read_code(p) >> 1, 1), :]
            return carry

        lax.fori_loop(0, SLOTS // UNROLL, one, 0)
        both = flip(rows_own[...].astype(BF16))
        return jnp.where((codes & 1) == 0, both[:MEMBERS], both[MEMBERS:])

    obs_left = near_copy(obs_out.at[0], obs_in.at[0], 2, left)
    obs_right = near_copy(obs_out.at[1], obs_in.at[1], 3, right)
    flip_block(0)
    obs_out[0] = gather(lambda p: smem_in[1, 0, p], code_in[1]).astype(BF16)
    obs_left.start()
    flip_block(BLOCKS - 1)
    obs_out[1] = gather(lambda p: smem_in[0, 0, p], code_in[0]).astype(BF16)
    obs_right.start()
    for j in range(1, BLOCKS - 1):
        flip_block(j)
    obs_own = gather(lambda p: smem_own[0, p], code_own[...])
    obs_left.wait()
    obs_right.wait()

    below = spot < HALO
    above = spot >= HALO + TILE
    observed = jnp.where(
        below,
        obs_in[1].astype(F32),
        jnp.where(above, obs_in[0].astype(F32), obs_own),
    )
    slot_id = lax.broadcasted_iota(jnp.int32, (1, SLOTS), 1)
    live = slot_id < count[0]
    live = live & jnp.logical_not(below & (me == 0))
    live = live & jnp.logical_not(above & (me == PEERS - 1))
    rate = jnp.where(live, weight[...], 0.0)
    obs_mean = jnp.sum(observed, axis=0, keepdims=True) * (1.0 / MEMBERS)
    spread = observed - obs_mean
    departure = value[...] - obs_mean
    scaled = spread * rate
    right_side = jnp.concatenate(
        [spread, jnp.broadcast_to(departure, (MEMBERS, SLOTS))], axis=0
    )
    gram_drive = lax.dot_general(
        scaled,
        right_side,
        (((1,), (1,)), ((), ())),
        precision=lax.Precision.HIGHEST,
        preferred_element_type=F32,
    )
    row_id = lax.broadcasted_iota(jnp.int32, (MEMBERS, 2 * MEMBERS), 0)
    col_id = lax.broadcasted_iota(jnp.int32, (MEMBERS, 2 * MEMBERS), 1)
    swapped = pltpu.roll(gram_drive, MEMBERS, 1)
    system = jnp.where(
        col_id < MEMBERS,
        jnp.where(row_id == col_id, gram_drive + (MEMBERS - 1.0), gram_drive),
        gram_drive - 0.5 * swapped,
    )

    def eliminate(i, system):
        sub = lax.broadcasted_iota(jnp.int32, (8, LANES), 0)

        def solve_pair(a, b, c, d):
            scale = 1.0 / (a * d - b * c)
            return lambda p, q: ((p * d - q * b) * scale, (q * a - p * c) * scale)

        for j in range(0, 8, 4):
            rows = [jnp.broadcast_to(system[0, j + r : j + r + 1, :], (8, LANES)) for r in range(4)]
            e = [[jnp.broadcast_to(r[:, j + k : j + k + 1], (8, LANES)) for k in range(4)] for r in rows]
            upper = solve_pair(e[0][0], e[0][1], e[1][0], e[1][1])
            new0, new1 = upper(rows[0], rows[1])
            u02, u12 = upper(e[0][2], e[1][2])
            u03, u13 = upper(e[0][3], e[1][3])
            low2 = rows[2] - e[2][0] * new0 - e[2][1] * new1
            low3 = rows[3] - e[3][0] * new0 - e[3][1] * new1
            lower = solve_pair(
                e[2][2] - e[2][0] * u02 - e[2][1] * u12,
                e[2][3] - e[2][0] * u03 - e[2][1] * u13,
                e[3][2] - e[3][0] * u02 - e[3][1] * u12,
                e[3][3] - e[3][0] * u03 - e[3][1] * u13,
            )
            new2, new3 = lower(low2, low3)
            new0 = new0 - u02 * new2 - u03 * new3
            new1 = new1 - u12 * new2 - u13 * new3
            rest = system
            for k, new in enumerate((new0, new1, new2, new3)):
                rest = rest - system[:, :, j + k : j + k + 1] * new
            first = rest[0]
            for k, new in enumerate((new0, new1, new2, new3)):
                first = jnp.where(sub == j + k, new, first)
            system = jnp.concatenate([first[None], rest[1:]], axis=0)
        system = jnp.concatenate([system[1:], system[:1]], axis=0)
        return pltpu.roll(system, LANES - 8, 2)

    system = lax.fori_loop(
        0, MEMBERS // 8, eliminate, system.reshape(MEMBERS // 8, 8, LANES)
    )
    mixing = system.reshape(MEMBERS, LANES)[:, :MEMBERS]
    mixing = mixing - jnp.sum(mixing, axis=0, keepdims=True) * (1.0 / MEMBERS)
    mixing_t = mixing.T
    coarse = mixing_t.astype(BF16)
    fine = (mixing_t - coarse.astype(F32)).astype(BF16)
    mixer = jnp.concatenate([coarse, fine], axis=1)

    def mix(j, channels):
        slabs = [state.at[j, c].reshape(MEMBERS, LANES)[...] for c in channels]
        slab = jnp.concatenate(slabs, axis=1)
        result = jnp.dot(
            mixer, jnp.concatenate([slab, slab], axis=0), preferred_element_type=F32
        ).astype(BF16)
        for k, c in enumerate(channels):
            mixed.at[j, c].reshape(MEMBERS, LANES)[...] = result[:, k * LANES : (k + 1) * LANES]

    def scatter_copy(j, low, high, target, tile):
        return pltpu.make_async_remote_copy(
            src_ref=mixed.at[j, low:high, target],
            dst_ref=out.at[low:high, :, tile_span(tile, j)],
            send_sem=exchange_sem.at[2],
            recv_sem=exchange_sem.at[3],
            device_id={"member": target},
            device_id_type=MESH,
        )

    def own_block(j):
        return pltpu.make_async_copy(
            mixed.at[j, 0:CH, me], out.at[:, :, tile_span(me, j)], local_sem.at[3 + j]
        )

    WIDE = 8
    for j, low, high in ((0, 0, 16), (0, 16, CH), (1, 0, CH), (2, 0, CH)):

        def mix_step(i, carry):
            mix(j, [i * WIDE + k for k in range(WIDE)])
            return carry

        lax.fori_loop(low // WIDE, -(-high // WIDE), mix_step, 0)

        def send_step(i, carry):
            scatter_copy(j, low, high, peer_of(me, i), me).start()
            return carry

        lax.fori_loop(1, PEERS, send_step, 0)
        if high == CH:
            own_block(j).start()

    all_members.wait_send()
    for j in range(BLOCKS):
        own_block(j).wait()
    others = out.at[:, :, 0 : (PEERS - 1) * TILE]
    pltpu.make_async_remote_copy(
        src_ref=others,
        dst_ref=others,
        send_sem=exchange_sem.at[2],
        recv_sem=exchange_sem.at[3],
        device_id={"member": left},
        device_id_type=MESH,
    ).wait()


def copy_kernel(source, target, held, sem):
    spans = [pl.ds(c, min(COPY_ROWS, CH - c)) for c in range(0, CH, COPY_ROWS)]
    arrive = [
        pltpu.make_async_copy(source.at[span], held.at[span], sem.at[0, k])
        for k, span in enumerate(spans)
    ]
    leave = [
        pltpu.make_async_copy(held.at[span], target.at[span], sem.at[1, k])
        for k, span in enumerate(spans)
    ]
    for copy in arrive:
        copy.start()
    for k, copy in enumerate(leave):
        arrive[k].wait()
        copy.start()
    for copy in leave:
        copy.wait()


def local(prior, w_up, w_down, site, count, value, weight):
    smem = pl.BlockSpec(memory_space=pltpu.SMEM)
    anywhere = pl.BlockSpec(memory_space=pl.ANY)
    members, channels, cells = prior.shape
    result = pl.pallas_call(
        kernel,
        out_shape=jax.ShapeDtypeStruct((channels, members, cells), BF16),
        in_specs=[anywhere] * 4 + [smem] + [anywhere] * 2,
        out_specs=anywhere,
        scratch_shapes=[
            pltpu.VMEM((CH, 2, HID), BF16),
            pltpu.VMEM((CH, 2, HID), BF16),
            pltpu.VMEM((1, SLOTS), jnp.int32),
            pltpu.VMEM((1, SLOTS), F32),
            pltpu.VMEM((1, SLOTS), F32),
            pltpu.VMEM((PEERS // 2, 2 * BLOCKS, FILL, 2, LANES), BF16),
            pltpu.VMEM((PEERS, BLOCKS, FILL, 2, LANES), BF16),
            pltpu.VMEM((BLOCKS, FILL, PEERS, 2, LANES), BF16),
            pltpu.VMEM((BLOCKS, FILL, PEERS, 2, LANES), BF16),
            pltpu.VMEM((BLOCKS * HALVES * LANES, LANES), F32),
            pltpu.VMEM((SLOTS, LANES), F32),
            pltpu.VMEM((2 * HID // LANES, 2 * LANES, LANES), F32),
            pltpu.VMEM((2, 2 * HID, 2 * LANES), BF16),
            pltpu.VMEM((2, 160, 2 * HID), BF16),
            pltpu.VMEM((1, SLOTS), jnp.int32),
            pltpu.VMEM((2, 1, SLOTS), jnp.int32),
            pltpu.VMEM((2, 1, SLOTS), jnp.int32),
            pltpu.SMEM((1, SLOTS), jnp.int32),
            pltpu.SMEM((2, 1, SLOTS), jnp.int32),
            pltpu.VMEM((2, MEMBERS, SLOTS), BF16),
            pltpu.VMEM((2, MEMBERS, SLOTS), BF16),
            pltpu.SemaphoreType.DMA((5,)),
            pltpu.SemaphoreType.DMA((2,)),
            pltpu.SemaphoreType.DMA((4,)),
            pltpu.SemaphoreType.DMA((4,)),
            pltpu.SemaphoreType.DMA((4,)),
            pltpu.SemaphoreType.DMA((3 + BLOCKS,)),
        ],
        compiler_params=pltpu.CompilerParams(
            collective_id=0, has_side_effects=True, vmem_limit_bytes=56 << 20
        ),
    )(
        prior.transpose(1, 0, 2),
        w_up.transpose(2, 0, 1),
        w_down.transpose(1, 0, 2),
        site,
        count,
        value,
        weight,
    )
    result = pl.pallas_call(
        copy_kernel,
        out_shape=jax.ShapeDtypeStruct(result.shape, BF16),
        in_specs=[anywhere],
        out_specs=anywhere,
        scratch_shapes=[pltpu.VMEM(result.shape, BF16), pltpu.SemaphoreType.DMA((2, 10))],
        compiler_params=pltpu.CompilerParams(vmem_limit_bytes=56 << 20),
    )(result)
    return result.transpose(1, 0, 2)


def solution(mesh):
    in_specs = (
        P("member", None, "space"),
        P(),
        P(),
        P(("member", "space"), None),
        P(("member", "space")),
        P(("member", "space"), None),
        P(("member", "space"), None),
    )
    return jax.shard_map(
        local,
        mesh=mesh,
        in_specs=in_specs,
        out_specs=P("member", None, "space"),
        check_vma=False,
    )
```

```python
import functools
import math

import jax
import jax.numpy as jnp
from jax import lax
from jax.experimental import pallas as pl
from jax.experimental.pallas import tpu as pltpu
from jax.sharding import PartitionSpec as P

MESH = pl.DeviceIdType.MESH
F32 = jnp.float32
BF16 = jnp.bfloat16

CH = 73
TILE = 384
HALO = 128
STRIP = TILE + 2 * HALO
SLOTS = 512
MEMBERS = 64
PEERS = 32
FILL = 80
PAIR = 152
HID = 512
LANES = 128
BLOCKS = TILE // LANES
ORDER = 23
OWN_STEP = 10
COPY_ROWS = 15
GROUP = 4
HALVES = 40
GELU_A = math.sqrt(2.0 / math.pi)
GELU_B = GELU_A * 0.044715


def peer_of(me, step):
    off = lax.rem(step * ORDER, PEERS)
    x = lax.rem(lax.rem(me, 4) + lax.rem(off, 4), 4)
    y = lax.rem(lax.rem(me // 4, 4) + lax.rem(off // 4, 4), 4)
    z = lax.rem(me // 16 + off // 16, 2)
    return z * 16 + y * 4 + x


def pair_of(me, i):
    turn = lax.rem(i + PEERS // 2 - OWN_STEP, PEERS // 2)
    tiles = []
    for t in range(2):
        x = lax.rem(lax.rem(me, 4) + lax.rem(turn, 4) + 2 * t, 4)
        y = lax.rem(lax.rem(me // 4, 4) + turn // 4 + 2 * t, 4)
        tiles.append(lax.rem(me // 16 + t, 2) * 16 + y * 4 + x)
    return tiles


def normalise(x):
    groups = x.reshape(PAIR // 8, 8, x.shape[1])

    def over_channels(group):
        group = group + pltpu.roll(group, 4, 0)
        return (group + pltpu.roll(group, 2, 0)) * (1.0 / CH)

    center = groups - over_channels(jnp.sum(groups, axis=0))[None]
    row = lax.broadcasted_iota(jnp.int32, center.shape[1:], 0)
    last = jnp.where(row < 2, center[PAIR // 8 - 1], 0.0)
    center = jnp.concatenate([center[: PAIR // 8 - 1], last[None]], axis=0)
    var = over_channels(jnp.sum(center * center, axis=0))
    return (center * lax.rsqrt(var + 1e-06)[None]).reshape(x.shape).astype(BF16)


def layer(x, w_up, w_down):
    lifted = jnp.dot(w_up, normalise(x), preferred_element_type=F32)
    bend = jnp.tanh(lifted * (GELU_A + GELU_B * (lifted * lifted)))
    twice_hidden = (lifted + lifted * bend).astype(BF16)
    return x + 0.5 * jnp.dot(w_down, twice_hidden, preferred_element_type=F32)


def kernel(
    prior,
    w_up_far,
    w_down_far,
    site_far,
    count,
    value_far,
    weight_far,
    out,
    w_up,
    w_down,
    site,
    value,
    weight,
    fields,
    msg,
    state,
    mixed,
    flipped,
    rows_own,
    spread_w,
    up,
    down,
    code_own,
    code_out,
    code_in,
    smem_own,
    smem_in,
    obs_out,
    obs_in,
    fetch_sem,
    load_sem,
    exchange_sem,
    near_send,
    near_recv,
    local_sem,
):
    fetches = [
        pltpu.make_async_copy(far, near, fetch_sem.at[k])
        for k, (far, near) in enumerate(
            (
                (site_far, site),
                (w_up_far, w_up),
                (w_down_far, w_down),
                (value_far, value),
                (weight_far, weight),
            )
        )
    ]
    for fetch in fetches:
        fetch.start()
    me = lax.axis_index("member")
    left = lax.rem(me + PEERS - 1, PEERS)
    right = lax.rem(me + 1, PEERS)

    def tile_span(tile, j):
        return pl.ds(pl.multiple_of(tile * TILE + j * LANES, LANES), LANES)

    def load_pair(i, sem):
        for t, tile in enumerate(pair_of(me, i)):
            for j in range(BLOCKS):
                pltpu.make_async_copy(
                    prior.at[:, :, tile_span(tile, j)],
                    fields.at[i, t * BLOCKS + j, 0:CH],
                    load_sem.at[sem],
                ).start()

    def loaded(i):
        block = fields.at[i, :, 0:CH]
        return pltpu.make_async_copy(block, block, load_sem.at[lax.rem(i, 2)])

    load_pair(0, 0)

    barrier = pltpu.get_barrier_semaphore()

    def greet(step, carry):
        pl.semaphore_signal(
            barrier, inc=1, device_id={"member": peer_of(me, step)}, device_id_type=MESH
        )
        return carry

    lax.fori_loop(1, PEERS, greet, 0)

    fetches[0].wait()
    sites = site[...]
    channel = ((sites >> 7) * 6554) >> 15
    spot = sites - channel * STRIP

    def code(cell):
        row = ((cell >> 7) * HALVES + (channel >> 1)) * LANES + (cell & (LANES - 1))
        return 2 * row + (channel & 1)

    code_own[...] = code(jnp.clip(spot - HALO, 0, TILE - 1))
    code_out[0] = code(jnp.minimum(spot, HALO - 1) + (TILE - HALO))
    code_out[1] = code(jnp.maximum(spot - (HALO + TILE), 0))

    own_codes = pltpu.make_async_copy(code_own, smem_own, local_sem.at[0])
    own_codes.start()

    state[:, CH:FILL] = jnp.zeros((BLOCKS, FILL - CH, PEERS, 2, LANES), BF16)

    spread_w[...] = jnp.zeros_like(spread_w)
    for fetch in fetches[1:]:
        fetch.wait()
    for source, l in ((w_up, 0), (w_down, 0), (w_up, 1), (w_down, 1)):
        plain = source[:, l, :].astype(F32)
        for m in range(2):
            for b in range(HID // LANES):
                spread_w[m * 4 + b, pl.ds(m, CH, stride=2), :] = plain[:, b * LANES : (b + 1) * LANES]
        for b in range(2 * HID // LANES):
            span = slice(b * LANES, (b + 1) * LANES)
            if source is w_up:
                up[l, span, :] = spread_w[b].T.astype(BF16)
            else:
                down[l, :, span] = spread_w[b, 0:160].astype(BF16)

    def near_copy(src, dst, sem, target):
        return pltpu.make_async_remote_copy(
            src_ref=src,
            dst_ref=dst,
            send_sem=near_send.at[sem],
            recv_sem=near_recv.at[sem],
            device_id={"member": target},
            device_id_type=MESH,
        )

    code_left = near_copy(code_out.at[0], code_in.at[0], 0, left)
    code_right = near_copy(code_out.at[1], code_in.at[1], 1, right)
    def gather_copy(target, source):
        return pltpu.make_async_remote_copy(
            src_ref=msg.at[target, :, 0:CH],
            dst_ref=state.at[:, 0:CH, source],
            send_sem=exchange_sem.at[0],
            recv_sem=exchange_sem.at[1],
            device_id={"member": target},
            device_id_type=MESH,
        )

    def forecast(i, tiles):
        row = lax.broadcasted_iota(jnp.int32, (PAIR, LANES), 0)
        blocks = []
        for b in range(2 * BLOCKS):
            block = fields.at[i, b].reshape(2 * FILL, LANES)[0:PAIR, :].astype(F32)
            blocks.append(jnp.where(row < 2 * CH, block, 0.0))
        x = jnp.concatenate(blocks, axis=1)
        for l in range(2):
            x = layer(x, up[l, :, 0:PAIR], down[l, 0:PAIR])
        fill = jnp.zeros((2 * FILL - PAIR, LANES), F32)
        for t, tile in enumerate(tiles):
            for j in range(BLOCKS):
                b = t * BLOCKS + j
                block = jnp.concatenate([x[:, b * LANES : (b + 1) * LANES], fill], axis=0)
                msg.at[tile, j].reshape(2 * FILL, LANES)[...] = block.astype(BF16)

    def forecast_step(i, carry):
        tiles = pair_of(me, i)

        @pl.when(i < PEERS // 2 - 1)
        def _():
            load_pair(i + 1, lax.rem(i + 1, 2))

        loaded(i).wait()
        forecast(i, tiles)

        @pl.when(i == 0)
        def _():
            pl.semaphore_wait(barrier, PEERS - 1)
            code_left.start()
            code_right.start()

        gather_copy(tiles[1], me).start()

        @pl.when(i != OWN_STEP)
        def _():
            gather_copy(tiles[0], me).start()

        return carry

    lax.fori_loop(0, PEERS // 2, forecast_step, 0)
    own_tile = pltpu.make_async_copy(msg.at[me, :, 0:CH], state.at[:, 0:CH, me], local_sem.at[1])
    own_tile.start()

    code_left.wait()
    code_right.wait()
    in_codes = pltpu.make_async_copy(code_in, smem_in, local_sem.at[2])
    in_codes.start()
    own_codes.wait()
    in_codes.wait()
    own_tile.wait()

    others = msg.at[0 : PEERS - 1, :, 0:CH]
    all_members = pltpu.make_async_remote_copy(
        src_ref=others,
        dst_ref=others,
        send_sem=exchange_sem.at[0],
        recv_sem=exchange_sem.at[1],
        device_id={"member": left},
        device_id_type=MESH,
    )
    all_members.wait_recv()

    def flip_block(j):
        def flip_step(g, carry):
            slabs = state.at[j, pl.ds(g * GROUP, GROUP)].reshape(GROUP * MEMBERS, LANES)[...]
            for h in range(GROUP // 2):
                base = pl.multiple_of((j * HALVES + g * (GROUP // 2) + h) * LANES, LANES)
                pair = slabs[h * LANES : (h + 1) * LANES]
                flipped[pl.ds(base, LANES), :] = pair.T.astype(F32)
            return carry

        lax.fori_loop(0, HALVES * 2 // GROUP, flip_step, 0, unroll=5)

    UNROLL = 16

    def gather(read_code, codes):
        def one(i, carry):
            for u in range(UNROLL):
                p = i * UNROLL + u
                rows_own[pl.ds(p, 1), :] = flipped[pl.ds(read_code(p) >> 1, 1), :]
            return carry

        lax.fori_loop(0, SLOTS // UNROLL, one, 0)
        both = jnp.concatenate(
            [
                rows_own[b * LANES : (b + 1) * LANES, :].astype(BF16).T
                for b in range(SLOTS // LANES)
            ],
            axis=1,
        ).astype(F32)
        return jnp.where((codes & 1) == 0, both[:MEMBERS], both[MEMBERS:])

    obs_left = near_copy(obs_out.at[0], obs_in.at[0], 2, left)
    obs_right = near_copy(obs_out.at[1], obs_in.at[1], 3, right)
    flip_block(0)
    obs_out[0] = gather(lambda p: smem_in[1, 0, p], code_in[1]).astype(BF16)
    obs_left.start()
    flip_block(BLOCKS - 1)
    obs_out[1] = gather(lambda p: smem_in[0, 0, p], code_in[0]).astype(BF16)
    obs_right.start()
    for j in range(1, BLOCKS - 1):
        flip_block(j)
    obs_own = gather(lambda p: smem_own[0, p], code_own[...])
    obs_left.wait()
    obs_right.wait()

    below = spot < HALO
    above = spot >= HALO + TILE
    observed = jnp.where(
        below,
        obs_in[1].astype(F32),
        jnp.where(above, obs_in[0].astype(F32), obs_own),
    )
    slot_id = lax.broadcasted_iota(jnp.int32, (1, SLOTS), 1)
    live = slot_id < count[0]
    live = live & jnp.logical_not(below & (me == 0))
    live = live & jnp.logical_not(above & (me == PEERS - 1))
    rate = jnp.where(live, weight[...], 0.0)
    obs_mean = jnp.sum(observed, axis=0, keepdims=True) * (1.0 / MEMBERS)
    spread = observed - obs_mean
    departure = value[...] - obs_mean
    scaled = spread * rate
    right_side = jnp.concatenate(
        [spread, jnp.broadcast_to(departure, (MEMBERS, SLOTS))], axis=0
    )
    gram_drive = lax.dot_general(
        scaled,
        right_side,
        (((1,), (1,)), ((), ())),
        precision=lax.Precision.HIGHEST,
        preferred_element_type=F32,
    )
    row_id = lax.broadcasted_iota(jnp.int32, (MEMBERS, 2 * MEMBERS), 0)
    col_id = lax.broadcasted_iota(jnp.int32, (MEMBERS, 2 * MEMBERS), 1)
    swapped = pltpu.roll(gram_drive, MEMBERS, 1)
    system = jnp.where(
        col_id < MEMBERS,
        jnp.where(row_id == col_id, gram_drive + (MEMBERS - 1.0), gram_drive),
        gram_drive - 0.5 * swapped,
    )

    def eliminate(i, system):
        sub = lax.broadcasted_iota(jnp.int32, (8, LANES), 0)

        def solve_pair(a, b, c, d):
            scale = 1.0 / (a * d - b * c)
            return lambda p, q: ((p * d - q * b) * scale, (q * a - p * c) * scale)

        for j in range(0, 8, 4):
            rows = [jnp.broadcast_to(system[0, j + r : j + r + 1, :], (8, LANES)) for r in range(4)]
            e = [[jnp.broadcast_to(r[:, j + k : j + k + 1], (8, LANES)) for k in range(4)] for r in rows]
            upper = solve_pair(e[0][0], e[0][1], e[1][0], e[1][1])
            new0, new1 = upper(rows[0], rows[1])
            u02, u12 = upper(e[0][2], e[1][2])
            u03, u13 = upper(e[0][3], e[1][3])
            low2 = rows[2] - e[2][0] * new0 - e[2][1] * new1
            low3 = rows[3] - e[3][0] * new0 - e[3][1] * new1
            lower = solve_pair(
                e[2][2] - e[2][0] * u02 - e[2][1] * u12,
                e[2][3] - e[2][0] * u03 - e[2][1] * u13,
                e[3][2] - e[3][0] * u02 - e[3][1] * u12,
                e[3][3] - e[3][0] * u03 - e[3][1] * u13,
            )
            new2, new3 = lower(low2, low3)
            new0 = new0 - u02 * new2 - u03 * new3
            new1 = new1 - u12 * new2 - u13 * new3
            rest = system
            for k, new in enumerate((new0, new1, new2, new3)):
                rest = rest - system[:, :, j + k : j + k + 1] * new
            first = rest[0]
            for k, new in enumerate((new0, new1, new2, new3)):
                first = jnp.where(sub == j + k, new, first)
            system = jnp.concatenate([first[None], rest[1:]], axis=0)
        system = jnp.concatenate([system[1:], system[:1]], axis=0)
        return pltpu.roll(system, LANES - 8, 2)

    system = lax.fori_loop(
        0, MEMBERS // 8, eliminate, system.reshape(MEMBERS // 8, 8, LANES)
    )
    mixing = system.reshape(MEMBERS, LANES)[:, :MEMBERS]
    mixing = mixing - jnp.sum(mixing, axis=0, keepdims=True) * (1.0 / MEMBERS)
    mixing_t = mixing.T
    coarse = mixing_t.astype(BF16)
    fine = (mixing_t - coarse.astype(F32)).astype(BF16)
    mixer = jnp.concatenate([coarse, fine], axis=1)

    def mix(j, channels):
        slabs = [state.at[j, c].reshape(MEMBERS, LANES)[...] for c in channels]
        slab = jnp.concatenate(slabs, axis=1)
        result = jnp.dot(
            mixer, jnp.concatenate([slab, slab], axis=0), preferred_element_type=F32
        ).astype(BF16)
        for k, c in enumerate(channels):
            mixed.at[j, c].reshape(MEMBERS, LANES)[...] = result[:, k * LANES : (k + 1) * LANES]

    def scatter_copy(j, low, high, target, tile):
        return pltpu.make_async_remote_copy(
            src_ref=mixed.at[j, low:high, target],
            dst_ref=out.at[low:high, :, tile_span(tile, j)],
            send_sem=exchange_sem.at[2],
            recv_sem=exchange_sem.at[3],
            device_id={"member": target},
            device_id_type=MESH,
        )

    def own_block(j):
        return pltpu.make_async_copy(
            mixed.at[j, 0:CH, me], out.at[:, :, tile_span(me, j)], local_sem.at[3 + j]
        )

    WIDE = 8
    for j, low, high in ((0, 0, 16), (0, 16, CH), (1, 0, CH), (2, 0, CH)):

        def mix_step(i, carry):
            mix(j, [i * WIDE + k for k in range(WIDE)])
            return carry

        lax.fori_loop(low // WIDE, -(-high // WIDE), mix_step, 0)

        def send_step(i, carry):
            scatter_copy(j, low, high, peer_of(me, i), me).start()
            return carry

        lax.fori_loop(1, PEERS, send_step, 0)
        if high == CH:
            own_block(j).start()

    all_members.wait_send()
    for j in range(BLOCKS):
        own_block(j).wait()
    others = out.at[:, :, 0 : (PEERS - 1) * TILE]
    pltpu.make_async_remote_copy(
        src_ref=others,
        dst_ref=others,
        send_sem=exchange_sem.at[2],
        recv_sem=exchange_sem.at[3],
        device_id={"member": left},
        device_id_type=MESH,
    ).wait()


def copy_kernel(source, target, held, sem):
    spans = [pl.ds(c, min(COPY_ROWS, CH - c)) for c in range(0, CH, COPY_ROWS)]
    arrive = [
        pltpu.make_async_copy(source.at[span], held.at[span], sem.at[0, k])
        for k, span in enumerate(spans)
    ]
    leave = [
        pltpu.make_async_copy(held.at[span], target.at[span], sem.at[1, k])
        for k, span in enumerate(spans)
    ]
    for copy in arrive:
        copy.start()
    for k, copy in enumerate(leave):
        arrive[k].wait()
        copy.start()
    for copy in leave:
        copy.wait()


def local(prior, w_up, w_down, site, count, value, weight):
    smem = pl.BlockSpec(memory_space=pltpu.SMEM)
    anywhere = pl.BlockSpec(memory_space=pl.ANY)
    members, channels, cells = prior.shape
    result = pl.pallas_call(
        kernel,
        out_shape=jax.ShapeDtypeStruct((channels, members, cells), BF16),
        in_specs=[anywhere] * 4 + [smem] + [anywhere] * 2,
        out_specs=anywhere,
        scratch_shapes=[
            pltpu.VMEM((CH, 2, HID), BF16),
            pltpu.VMEM((CH, 2, HID), BF16),
            pltpu.VMEM((1, SLOTS), jnp.int32),
            pltpu.VMEM((1, SLOTS), F32),
            pltpu.VMEM((1, SLOTS), F32),
            pltpu.VMEM((PEERS // 2, 2 * BLOCKS, FILL, 2, LANES), BF16),
            pltpu.VMEM((PEERS, BLOCKS, FILL, 2, LANES), BF16),
            pltpu.VMEM((BLOCKS, FILL, PEERS, 2, LANES), BF16),
            pltpu.VMEM((BLOCKS, FILL, PEERS, 2, LANES), BF16),
            pltpu.VMEM((BLOCKS * HALVES * LANES, LANES), F32),
            pltpu.VMEM((SLOTS, LANES), F32),
            pltpu.VMEM((2 * HID // LANES, 2 * LANES, LANES), F32),
            pltpu.VMEM((2, 2 * HID, 2 * LANES), BF16),
            pltpu.VMEM((2, 160, 2 * HID), BF16),
            pltpu.VMEM((1, SLOTS), jnp.int32),
            pltpu.VMEM((2, 1, SLOTS), jnp.int32),
            pltpu.VMEM((2, 1, SLOTS), jnp.int32),
            pltpu.SMEM((1, SLOTS), jnp.int32),
            pltpu.SMEM((2, 1, SLOTS), jnp.int32),
            pltpu.VMEM((2, MEMBERS, SLOTS), BF16),
            pltpu.VMEM((2, MEMBERS, SLOTS), BF16),
            pltpu.SemaphoreType.DMA((5,)),
            pltpu.SemaphoreType.DMA((2,)),
            pltpu.SemaphoreType.DMA((4,)),
            pltpu.SemaphoreType.DMA((4,)),
            pltpu.SemaphoreType.DMA((4,)),
            pltpu.SemaphoreType.DMA((3 + BLOCKS,)),
        ],
        compiler_params=pltpu.CompilerParams(
            collective_id=0, has_side_effects=True, vmem_limit_bytes=56 << 20
        ),
    )(
        prior.transpose(1, 0, 2),
        w_up.transpose(2, 0, 1),
        w_down.transpose(1, 0, 2),
        site,
        count,
        value,
        weight,
    )
    result = pl.pallas_call(
        copy_kernel,
        out_shape=jax.ShapeDtypeStruct(result.shape, BF16),
        in_specs=[anywhere],
        out_specs=anywhere,
        scratch_shapes=[pltpu.VMEM(result.shape, BF16), pltpu.SemaphoreType.DMA((2, 10))],
        compiler_params=pltpu.CompilerParams(vmem_limit_bytes=56 << 20),
    )(result)
    return result.transpose(1, 0, 2)


def solution(mesh):
    in_specs = (
        P("member", None, "space"),
        P(),
        P(),
        P(("member", "space"), None),
        P(("member", "space")),
        P(("member", "space"), None),
        P(("member", "space"), None),
    )
    return jax.shard_map(
        local,
        mesh=mesh,
        in_specs=in_specs,
        out_specs=P("member", None, "space"),
        check_vma=False,
    )
```

```python
import functools
import math

import jax
import jax.numpy as jnp
from jax import lax
from jax.experimental import pallas as pl
from jax.experimental.pallas import tpu as pltpu
from jax.sharding import PartitionSpec as P

MESH = pl.DeviceIdType.MESH
F32 = jnp.float32
BF16 = jnp.bfloat16

CH = 73
TILE = 384
HALO = 128
STRIP = TILE + 2 * HALO
SLOTS = 512
MEMBERS = 64
PEERS = 32
FILL = 80
PAIR = 152
HID = 512
LANES = 128
BLOCKS = TILE // LANES
ORDER = 23
OWN_STEP = 10
COPY_ROWS = 15
GROUP = 4
HALVES = 40
GELU_A = math.sqrt(2.0 / math.pi)
GELU_B = GELU_A * 0.044715


def peer_of(me, step):
    off = lax.rem(step * ORDER, PEERS)
    x = lax.rem(lax.rem(me, 4) + lax.rem(off, 4), 4)
    y = lax.rem(lax.rem(me // 4, 4) + lax.rem(off // 4, 4), 4)
    z = lax.rem(me // 16 + off // 16, 2)
    return z * 16 + y * 4 + x


def pair_of(me, i):
    turn = lax.rem(i + PEERS // 2 - OWN_STEP, PEERS // 2)
    tiles = []
    for t in range(2):
        x = lax.rem(lax.rem(me, 4) + lax.rem(turn, 4) + 2 * t, 4)
        y = lax.rem(lax.rem(me // 4, 4) + turn // 4 + 2 * t, 4)
        tiles.append(lax.rem(me // 16 + t, 2) * 16 + y * 4 + x)
    return tiles


def normalise(x):
    groups = x.reshape(PAIR // 8, 8, x.shape[1])

    def over_channels(group):
        group = group + pltpu.roll(group, 4, 0)
        return (group + pltpu.roll(group, 2, 0)) * (1.0 / CH)

    center = groups - over_channels(jnp.sum(groups, axis=0))[None]
    row = lax.broadcasted_iota(jnp.int32, center.shape[1:], 0)
    last = jnp.where(row < 2, center[PAIR // 8 - 1], 0.0)
    center = jnp.concatenate([center[: PAIR // 8 - 1], last[None]], axis=0)
    var = over_channels(jnp.sum(center * center, axis=0))
    return (center * lax.rsqrt(var + 1e-06)[None]).reshape(x.shape).astype(BF16)


def layer(x, w_up, w_down):
    lifted = jnp.dot(w_up, normalise(x), preferred_element_type=F32)
    bend = jnp.tanh(lifted * (GELU_A + GELU_B * (lifted * lifted)))
    twice_hidden = (lifted + lifted * bend).astype(BF16)
    return x + 0.5 * jnp.dot(w_down, twice_hidden, preferred_element_type=F32)


def kernel(
    prior,
    w_up_far,
    w_down_far,
    site_far,
    count,
    value_far,
    weight_far,
    out,
    w_up,
    w_down,
    site,
    value,
    weight,
    fields,
    msg,
    state,
    mixed,
    flipped,
    rows_own,
    spread_w,
    up,
    down,
    code_own,
    code_out,
    code_in,
    smem_own,
    smem_in,
    obs_out,
    obs_in,
    fetch_sem,
    load_sem,
    exchange_sem,
    near_send,
    near_recv,
    local_sem,
):
    fetches = [
        pltpu.make_async_copy(far, near, fetch_sem.at[k])
        for k, (far, near) in enumerate(
            (
                (site_far, site),
                (w_up_far, w_up),
                (w_down_far, w_down),
                (value_far, value),
                (weight_far, weight),
            )
        )
    ]
    for fetch in fetches:
        fetch.start()
    me = lax.axis_index("member")
    left = lax.rem(me + PEERS - 1, PEERS)
    right = lax.rem(me + 1, PEERS)

    def tile_span(tile, j):
        return pl.ds(pl.multiple_of(tile * TILE + j * LANES, LANES), LANES)

    def load_pair(i, sem):
        for t, tile in enumerate(pair_of(me, i)):
            for j in range(BLOCKS):
                pltpu.make_async_copy(
                    prior.at[:, :, tile_span(tile, j)],
                    fields.at[i, t * BLOCKS + j, 0:CH],
                    load_sem.at[sem],
                ).start()

    def loaded(i):
        block = fields.at[i, :, 0:CH]
        return pltpu.make_async_copy(block, block, load_sem.at[lax.rem(i, 2)])

    load_pair(0, 0)

    barrier = pltpu.get_barrier_semaphore()

    def greet(step, carry):
        pl.semaphore_signal(
            barrier, inc=1, device_id={"member": peer_of(me, step)}, device_id_type=MESH
        )
        return carry

    lax.fori_loop(1, PEERS, greet, 0)

    fetches[0].wait()
    sites = site[...]
    channel = ((sites >> 7) * 6554) >> 15
    spot = sites - channel * STRIP

    def code(cell):
        row = ((cell >> 7) * HALVES + (channel >> 1)) * LANES + (cell & (LANES - 1))
        return 2 * row + (channel & 1)

    code_own[...] = code(jnp.clip(spot - HALO, 0, TILE - 1))
    code_out[0] = code(jnp.minimum(spot, HALO - 1) + (TILE - HALO))
    code_out[1] = code(jnp.maximum(spot - (HALO + TILE), 0))

    own_codes = pltpu.make_async_copy(code_own, smem_own, local_sem.at[0])
    own_codes.start()

    state[:, CH:FILL] = jnp.zeros((BLOCKS, FILL - CH, PEERS, 2, LANES), BF16)

    spread_w[...] = jnp.zeros_like(spread_w)
    for fetch in fetches[1:]:
        fetch.wait()
    for source, l in ((w_up, 0), (w_down, 0), (w_up, 1), (w_down, 1)):
        plain = source[:, l, :].astype(F32)
        for m in range(2):
            for b in range(HID // LANES):
                spread_w[m * 4 + b, pl.ds(m, CH, stride=2), :] = plain[:, b * LANES : (b + 1) * LANES]
        for b in range(2 * HID // LANES):
            span = slice(b * LANES, (b + 1) * LANES)
            if source is w_up:
                up[l, span, :] = spread_w[b].T.astype(BF16)
            else:
                down[l, :, span] = spread_w[b, 0:160].astype(BF16)

    def near_copy(src, dst, sem, target):
        return pltpu.make_async_remote_copy(
            src_ref=src,
            dst_ref=dst,
            send_sem=near_send.at[sem],
            recv_sem=near_recv.at[sem],
            device_id={"member": target},
            device_id_type=MESH,
        )

    code_left = near_copy(code_out.at[0], code_in.at[0], 0, left)
    code_right = near_copy(code_out.at[1], code_in.at[1], 1, right)
    def gather_copy(target, source):
        return pltpu.make_async_remote_copy(
            src_ref=msg.at[target, :, 0:CH],
            dst_ref=state.at[:, 0:CH, source],
            send_sem=exchange_sem.at[0],
            recv_sem=exchange_sem.at[1],
            device_id={"member": target},
            device_id_type=MESH,
        )

    def forecast(i, tiles):
        row = lax.broadcasted_iota(jnp.int32, (PAIR, LANES), 0)
        blocks = []
        for b in range(2 * BLOCKS):
            block = fields.at[i, b].reshape(2 * FILL, LANES)[0:PAIR, :].astype(F32)
            blocks.append(jnp.where(row < 2 * CH, block, 0.0))
        x = jnp.concatenate(blocks, axis=1)
        for l in range(2):
            x = layer(x, up[l, :, 0:PAIR], down[l, 0:PAIR])
        fill = jnp.zeros((2 * FILL - PAIR, LANES), F32)
        for t, tile in enumerate(tiles):
            for j in range(BLOCKS):
                b = t * BLOCKS + j
                block = jnp.concatenate([x[:, b * LANES : (b + 1) * LANES], fill], axis=0)
                msg.at[tile, j].reshape(2 * FILL, LANES)[...] = block.astype(BF16)

    def forecast_step(i, carry):
        tiles = pair_of(me, i)

        @pl.when(i < PEERS // 2 - 1)
        def _():
            load_pair(i + 1, lax.rem(i + 1, 2))

        loaded(i).wait()
        forecast(i, tiles)

        @pl.when(i == 0)
        def _():
            pl.semaphore_wait(barrier, PEERS - 1)
            code_left.start()
            code_right.start()

        gather_copy(tiles[1], me).start()

        @pl.when(i != OWN_STEP)
        def _():
            gather_copy(tiles[0], me).start()

        return carry

    lax.fori_loop(0, PEERS // 2, forecast_step, 0)
    own_tile = pltpu.make_async_copy(msg.at[me, :, 0:CH], state.at[:, 0:CH, me], local_sem.at[1])
    own_tile.start()

    code_left.wait()
    code_right.wait()
    in_codes = pltpu.make_async_copy(code_in, smem_in, local_sem.at[2])
    in_codes.start()
    own_codes.wait()
    in_codes.wait()
    own_tile.wait()

    others = msg.at[0 : PEERS - 1, :, 0:CH]
    all_members = pltpu.make_async_remote_copy(
        src_ref=others,
        dst_ref=others,
        send_sem=exchange_sem.at[0],
        recv_sem=exchange_sem.at[1],
        device_id={"member": left},
        device_id_type=MESH,
    )
    all_members.wait_recv()

    def flip_block(j):
        def flip_step(g, carry):
            slabs = state.at[j, pl.ds(g * GROUP, GROUP)].reshape(GROUP * MEMBERS, LANES)[...]
            for h in range(GROUP // 2):
                base = pl.multiple_of((j * HALVES + g * (GROUP // 2) + h) * LANES, LANES)
                pair = slabs[h * LANES : (h + 1) * LANES]
                flipped[pl.ds(base, LANES), :] = pair.T.astype(F32)
            return carry

        lax.fori_loop(0, HALVES * 2 // GROUP, flip_step, 0, unroll=5)

    UNROLL = 32

    def gather(read_code, codes):
        def one(i, carry):
            for u in range(UNROLL):
                p = i * UNROLL + u
                rows_own[pl.ds(p, 1), :] = flipped[pl.ds(read_code(p) >> 1, 1), :]
            return carry

        lax.fori_loop(0, SLOTS // UNROLL, one, 0)
        both = jnp.concatenate(
            [
                rows_own[b * LANES : (b + 1) * LANES, :].astype(BF16).T
                for b in range(SLOTS // LANES)
            ],
            axis=1,
        ).astype(F32)
        return jnp.where((codes & 1) == 0, both[:MEMBERS], both[MEMBERS:])

    obs_left = near_copy(obs_out.at[0], obs_in.at[0], 2, left)
    obs_right = near_copy(obs_out.at[1], obs_in.at[1], 3, right)
    flip_block(0)
    obs_out[0] = gather(lambda p: smem_in[1, 0, p], code_in[1]).astype(BF16)
    obs_left.start()
    flip_block(BLOCKS - 1)
    obs_out[1] = gather(lambda p: smem_in[0, 0, p], code_in[0]).astype(BF16)
    obs_right.start()
    for j in range(1, BLOCKS - 1):
        flip_block(j)
    obs_own = gather(lambda p: smem_own[0, p], code_own[...])
    obs_left.wait()
    obs_right.wait()

    below = spot < HALO
    above = spot >= HALO + TILE
    observed = jnp.where(
        below,
        obs_in[1].astype(F32),
        jnp.where(above, obs_in[0].astype(F32), obs_own),
    )
    slot_id = lax.broadcasted_iota(jnp.int32, (1, SLOTS), 1)
    live = slot_id < count[0]
    live = live & jnp.logical_not(below & (me == 0))
    live = live & jnp.logical_not(above & (me == PEERS - 1))
    rate = jnp.where(live, weight[...], 0.0)
    obs_mean = jnp.sum(observed, axis=0, keepdims=True) * (1.0 / MEMBERS)
    spread = observed - obs_mean
    departure = value[...] - obs_mean
    scaled = spread * rate
    right_side = jnp.concatenate(
        [spread, jnp.broadcast_to(departure, (MEMBERS, SLOTS))], axis=0
    )
    gram_drive = lax.dot_general(
        scaled,
        right_side,
        (((1,), (1,)), ((), ())),
        precision=lax.Precision.HIGHEST,
        preferred_element_type=F32,
    )
    row_id = lax.broadcasted_iota(jnp.int32, (MEMBERS, 2 * MEMBERS), 0)
    col_id = lax.broadcasted_iota(jnp.int32, (MEMBERS, 2 * MEMBERS), 1)
    swapped = pltpu.roll(gram_drive, MEMBERS, 1)
    system = jnp.where(
        col_id < MEMBERS,
        jnp.where(row_id == col_id, gram_drive + (MEMBERS - 1.0), gram_drive),
        gram_drive - 0.5 * swapped,
    )

    def eliminate(i, system):
        sub = lax.broadcasted_iota(jnp.int32, (8, LANES), 0)

        def solve_pair(a, b, c, d):
            scale = 1.0 / (a * d - b * c)
            return lambda p, q: ((p * d - q * b) * scale, (q * a - p * c) * scale)

        for j in range(0, 8, 4):
            rows = [jnp.broadcast_to(system[0, j + r : j + r + 1, :], (8, LANES)) for r in range(4)]
            e = [[jnp.broadcast_to(r[:, j + k : j + k + 1], (8, LANES)) for k in range(4)] for r in rows]
            upper = solve_pair(e[0][0], e[0][1], e[1][0], e[1][1])
            new0, new1 = upper(rows[0], rows[1])
            u02, u12 = upper(e[0][2], e[1][2])
            u03, u13 = upper(e[0][3], e[1][3])
            low2 = rows[2] - e[2][0] * new0 - e[2][1] * new1
            low3 = rows[3] - e[3][0] * new0 - e[3][1] * new1
            lower = solve_pair(
                e[2][2] - e[2][0] * u02 - e[2][1] * u12,
                e[2][3] - e[2][0] * u03 - e[2][1] * u13,
                e[3][2] - e[3][0] * u02 - e[3][1] * u12,
                e[3][3] - e[3][0] * u03 - e[3][1] * u13,
            )
            new2, new3 = lower(low2, low3)
            new0 = new0 - u02 * new2 - u03 * new3
            new1 = new1 - u12 * new2 - u13 * new3
            rest = system
            for k, new in enumerate((new0, new1, new2, new3)):
                rest = rest - system[:, :, j + k : j + k + 1] * new
            first = rest[0]
            for k, new in enumerate((new0, new1, new2, new3)):
                first = jnp.where(sub == j + k, new, first)
            system = jnp.concatenate([first[None], rest[1:]], axis=0)
        system = jnp.concatenate([system[1:], system[:1]], axis=0)
        return pltpu.roll(system, LANES - 8, 2)

    system = lax.fori_loop(
        0, MEMBERS // 8, eliminate, system.reshape(MEMBERS // 8, 8, LANES)
    )
    mixing = system.reshape(MEMBERS, LANES)[:, :MEMBERS]
    mixing = mixing - jnp.sum(mixing, axis=0, keepdims=True) * (1.0 / MEMBERS)
    mixing_t = mixing.T
    coarse = mixing_t.astype(BF16)
    fine = (mixing_t - coarse.astype(F32)).astype(BF16)
    mixer = jnp.concatenate([coarse, fine], axis=1)

    def mix(j, channels):
        slabs = [state.at[j, c].reshape(MEMBERS, LANES)[...] for c in channels]
        slab = jnp.concatenate(slabs, axis=1)
        result = jnp.dot(
            mixer, jnp.concatenate([slab, slab], axis=0), preferred_element_type=F32
        ).astype(BF16)
        for k, c in enumerate(channels):
            mixed.at[j, c].reshape(MEMBERS, LANES)[...] = result[:, k * LANES : (k + 1) * LANES]

    def scatter_copy(j, low, high, target, tile):
        return pltpu.make_async_remote_copy(
            src_ref=mixed.at[j, low:high, target],
            dst_ref=out.at[low:high, :, tile_span(tile, j)],
            send_sem=exchange_sem.at[2],
            recv_sem=exchange_sem.at[3],
            device_id={"member": target},
            device_id_type=MESH,
        )

    def own_block(j):
        return pltpu.make_async_copy(
            mixed.at[j, 0:CH, me], out.at[:, :, tile_span(me, j)], local_sem.at[3 + j]
        )

    WIDE = 8
    for j, low, high in ((0, 0, 16), (0, 16, CH), (1, 0, CH), (2, 0, CH)):

        def mix_step(i, carry):
            mix(j, [i * WIDE + k for k in range(WIDE)])
            return carry

        lax.fori_loop(low // WIDE, -(-high // WIDE), mix_step, 0, unroll=2)

        def send_step(i, carry):
            tiles = pair_of(me, i)
            scatter_copy(j, low, high, tiles[1], me).start()

            @pl.when(i != OWN_STEP)
            def _():
                scatter_copy(j, low, high, tiles[0], me).start()

            return carry

        lax.fori_loop(0, PEERS // 2, send_step, 0)
        if high == CH:
            own_block(j).start()

    all_members.wait_send()
    for j in range(BLOCKS):
        own_block(j).wait()
    others = out.at[:, :, 0 : (PEERS - 1) * TILE]
    pltpu.make_async_remote_copy(
        src_ref=others,
        dst_ref=others,
        send_sem=exchange_sem.at[2],
        recv_sem=exchange_sem.at[3],
        device_id={"member": left},
        device_id_type=MESH,
    ).wait()


def copy_kernel(source, target, held, sem):
    spans = [pl.ds(c, min(COPY_ROWS, CH - c)) for c in range(0, CH, COPY_ROWS)]
    arrive = [
        pltpu.make_async_copy(source.at[span], held.at[span], sem.at[0, k])
        for k, span in enumerate(spans)
    ]
    leave = [
        pltpu.make_async_copy(held.at[span], target.at[span], sem.at[1, k])
        for k, span in enumerate(spans)
    ]
    for copy in arrive:
        copy.start()
    for k, copy in enumerate(leave):
        arrive[k].wait()
        copy.start()
    for copy in leave:
        copy.wait()


def local(prior, w_up, w_down, site, count, value, weight):
    smem = pl.BlockSpec(memory_space=pltpu.SMEM)
    anywhere = pl.BlockSpec(memory_space=pl.ANY)
    members, channels, cells = prior.shape
    result = pl.pallas_call(
        kernel,
        out_shape=jax.ShapeDtypeStruct((channels, members, cells), BF16),
        in_specs=[anywhere] * 4 + [smem] + [anywhere] * 2,
        out_specs=anywhere,
        scratch_shapes=[
            pltpu.VMEM((CH, 2, HID), BF16),
            pltpu.VMEM((CH, 2, HID), BF16),
            pltpu.VMEM((1, SLOTS), jnp.int32),
            pltpu.VMEM((1, SLOTS), F32),
            pltpu.VMEM((1, SLOTS), F32),
            pltpu.VMEM((PEERS // 2, 2 * BLOCKS, FILL, 2, LANES), BF16),
            pltpu.VMEM((PEERS, BLOCKS, FILL, 2, LANES), BF16),
            pltpu.VMEM((BLOCKS, FILL, PEERS, 2, LANES), BF16),
            pltpu.VMEM((BLOCKS, FILL, PEERS, 2, LANES), BF16),
            pltpu.VMEM((BLOCKS * HALVES * LANES, LANES), F32),
            pltpu.VMEM((SLOTS, LANES), F32),
            pltpu.VMEM((2 * HID // LANES, 2 * LANES, LANES), F32),
            pltpu.VMEM((2, 2 * HID, 2 * LANES), BF16),
            pltpu.VMEM((2, 160, 2 * HID), BF16),
            pltpu.VMEM((1, SLOTS), jnp.int32),
            pltpu.VMEM((2, 1, SLOTS), jnp.int32),
            pltpu.VMEM((2, 1, SLOTS), jnp.int32),
            pltpu.SMEM((1, SLOTS), jnp.int32),
            pltpu.SMEM((2, 1, SLOTS), jnp.int32),
            pltpu.VMEM((2, MEMBERS, SLOTS), BF16),
            pltpu.VMEM((2, MEMBERS, SLOTS), BF16),
            pltpu.SemaphoreType.DMA((5,)),
            pltpu.SemaphoreType.DMA((2,)),
            pltpu.SemaphoreType.DMA((4,)),
            pltpu.SemaphoreType.DMA((4,)),
            pltpu.SemaphoreType.DMA((4,)),
            pltpu.SemaphoreType.DMA((3 + BLOCKS,)),
        ],
        compiler_params=pltpu.CompilerParams(
            collective_id=0, has_side_effects=True, vmem_limit_bytes=56 << 20
        ),
    )(
        prior.transpose(1, 0, 2),
        w_up.transpose(2, 0, 1),
        w_down.transpose(1, 0, 2),
        site,
        count,
        value,
        weight,
    )
    result = pl.pallas_call(
        copy_kernel,
        out_shape=jax.ShapeDtypeStruct(result.shape, BF16),
        in_specs=[anywhere],
        out_specs=anywhere,
        scratch_shapes=[pltpu.VMEM(result.shape, BF16), pltpu.SemaphoreType.DMA((2, 10))],
        compiler_params=pltpu.CompilerParams(vmem_limit_bytes=56 << 20),
    )(result)
    return result.transpose(1, 0, 2)


def solution(mesh):
    in_specs = (
        P("member", None, "space"),
        P(),
        P(),
        P(("member", "space"), None),
        P(("member", "space")),
        P(("member", "space"), None),
        P(("member", "space"), None),
    )
    return jax.shard_map(
        local,
        mesh=mesh,
        in_specs=in_specs,
        out_specs=P("member", None, "space"),
        check_vma=False,
    )
```
